32 devices in a mesh: dp: 8 (over z, y), expert: 4 (over x, core).
Axes of the slice: x: 2, y: 2, z: 4, core: 2. Of those that a mesh axis runs over, the one named last changes fastest.
Arguments:
- tokens: bfloat16 [16384, 768], P(('dp', 'expert')), may hold values from -6 to 6
- assigned: int32 [16384, 1], P(('dp', 'expert')), may hold values from 0 to 3; in each aligned block of 512 rows (0 to 511, 512 to 1023, ...) at most 256 rows name the same one
- gate_prob: float32 [16384, 1], P(('dp', 'expert')), may hold values from 0.2 to 1
- cotangent: bfloat16 [16384, 768], P(('dp', 'expert')), may hold values from -6 to 6
- weight_in: bfloat16 [4, 768, 3072], P('expert'), may hold values from -0.21875 to 0.21875
- weight_out: bfloat16 [4, 3072, 768], P('expert'), may hold values from -0.109375 to 0.109375
- moment_in: float32 [4, 768, 3072], P('expert', 'dp'), may hold values from -60 to 60
- moment_out: float32 [4, 3072, 768], P('expert', 'dp'), may hold values from -60 to 60
- second_in: float32 [4, 768, 3072], P('expert', 'dp'), may hold values from 1 to 1000
- second_out: float32 [4, 3072, 768], P('expert', 'dp'), may hold values from 1 to 1000
Outputs:
- combined: bfloat16 [16384, 768], P(('dp', 'expert'))
- new_weight_in: float32 [4, 768, 3072], P('expert', 'dp')
- new_weight_out: float32 [4, 3072, 768], P('expert', 'dp')
- new_moment_in: float32 [4, 768, 3072], P('expert', 'dp')
- new_moment_out: float32 [4, 3072, 768], P('expert', 'dp')
- new_second_in: float32 [4, 768, 3072], P('expert', 'dp')
- new_second_out: float32 [4, 3072, 768], P('expert', 'dp')
The draws below stay inside these ranges and needn't reach their ends.
Inputs may be any that keep to these rules, and one draw needn't show every extreme that they name: `assigned`: within each device's 512 rows (aligned blocks), no expert is named more than 256 times, a bound that some block reaches; every expert is named somewhere.
All inputs are finite; a program needn't handle non-finite values.
Results may differ from the reference program's by a relative error of at most 0.0012.
The reference program's roundings to bfloat16 on the way (of `scaled`, `hidden`, `expert_out` and `hidden_grad`) count: a program that leaves them out, or rounds other values in their place, can miss the bound.
Values may be sent and summed in bfloat16 or wider, within the bound.
No kernel may reach another device: no remote copies, remote signals or barrier semaphores. Data moves between devices by JAX's collectives and lax.ppermute only.
A program may use at most 192 MiB of HBM per device.

```python
import math
import jax
import jax.numpy as jnp
import numpy as np
from jax import lax

D = 768
FF = 3072
TOK_DEV = 512
EXPERTS = 4
CAP = 256
TOKENS = 16384
LEVELS = 3
N_DP = 8
N_EXPERT = 4


def replica_owner():
    return jnp.arange(TOKENS, dtype=jnp.int32) // (TOKENS // N_DP)


def row_noise(key):
    return jnp.clip(jax.random.normal(key, (TOKENS, D), jnp.float32), -5.0, 5.0)


def draw_tokens(key, part):
    keys = jax.random.split(jax.random.fold_in(key, 11), 3)
    feature_pos = jnp.arange(D, dtype=jnp.float32) / D
    envelope = 0.2 + 2.8 * feature_pos * feature_pos
    common = envelope * jnp.clip(jax.random.normal(keys[0], (D,), jnp.float32), -2.0, 2.0)
    strength = jax.random.uniform(keys[1], (N_DP,), jnp.float32, 0.3, 1.2)
    owner = replica_owner()
    values = strength[owner][:, None] * common[None, :] + row_noise(keys[2])
    return jnp.clip(values, -6.0, 6.0).astype(jnp.bfloat16)


def draw_cotangent(key, part):
    keys = jax.random.split(jax.random.fold_in(key, 23), 3)
    common = jnp.clip(jax.random.normal(keys[0], (D,), jnp.float32), -3.0, 3.0)
    low_end = -3.912023
    high_end = -0.9162907
    strength = jnp.exp(jax.random.uniform(keys[1], (N_DP,), jnp.float32, low_end, high_end))
    owner = replica_owner()
    values = strength[owner][:, None] * common[None, :] + row_noise(keys[2])
    return jnp.clip(values, -6.0, 6.0).astype(jnp.bfloat16)


def shard_levels(stream_key, shape, cuts, low, top_value):
    factor_of, own = 1.0, jax.random.fold_in(stream_key, 6)
    for axis_at, parts in cuts:
        heights = jnp.exp(jax.random.uniform(jax.random.fold_in(own, axis_at), (parts,), jnp.float32, low / len(cuts), top_value / len(cuts)))
        factor_of = factor_of * jnp.repeat(heights, shape[axis_at] // parts).reshape([-1 if axis == axis_at else 1 for axis in range(len(shape))])
    return factor_of


def assign_block(own_key, own, number, rows, number_of, top, bound, slope):
    ranking = jax.random.permutation(own_key, number_of)
    crowded, usual = shares(number_of, rows * top, bound, slope, True), shares(number_of, rows * top, bound, slope, False)
    places = jnp.arange(number_of)

    def named(sizes, turn):
        used = int((sizes > 0).sum())
        fixed = max(1, used // 4)
        shifted = fixed + (places - fixed + turn * (used - fixed)) % max(1, number_of - fixed)
        return jnp.zeros((number_of,), jnp.int32).at[ranking[jnp.where(places < fixed, places, shifted)]].set(jnp.asarray(sizes, jnp.int32))

    sizes = jnp.where(number % 4 == 0, named(crowded, number // 4), named(usual, number - number // 4 - 1))
    mixed = jax.random.permutation(jax.random.fold_in(own, 3), number_of)
    source_of, sink = mixed[0:number_of // 2 * 2:2], mixed[1:number_of // 2 * 2:2]
    room = jnp.minimum(sizes[source_of] - 1, bound - sizes[sink]) // 2
    room = jnp.where((source_of == ranking[0]) | (sink == ranking[0]) | (sizes[sink] == 0), 0, jnp.maximum(room, 0))
    shifted = jax.random.randint(jax.random.fold_in(own, 4), (number_of // 2,), 0, 1 << 20) % (room + 1)
    sizes = sizes.at[source_of].add(-shifted).at[sink].add(shifted)
    items = jnp.searchsorted(jnp.cumsum(sizes), jnp.arange(rows * top), side="right").astype(jnp.int32)
    table = items.reshape(top, rows).T
    table = table[jax.random.permutation(jax.random.fold_in(own, 1), rows)]
    turn = jax.random.randint(jax.random.fold_in(own, 2), (rows, 1), 0, top)
    return jnp.take_along_axis(table, (jnp.arange(top)[None, :] + turn) % top, axis=1)


def shares(count, total, most, lean, full):
    loads = [(1 << 20) // math.isqrt(grade ** lean) + 1 for grade in range(1, count + 1)]
    largest = most if full else min(most, max(-(-total // count), total * loads[0] // sum(loads)))
    least = 1 if total - largest >= count - 1 else 0
    given, rest = [largest] + [least] * (count - 1), total - largest - least * (count - 1)
    while rest > 0:
        movable = [i for i in range(1, count) if given[i] < largest] or [i for i in range(1, count) if given[i] < most]
        mass, budget = sum([loads[i] for i in movable]), rest
        for i in movable:
            more = min(most - given[i], max(1, budget * loads[i] // mass), rest)
            given[i] = given[i] + more
            rest = rest - more
    return np.array(given)


def gaussian(own_key, shape, width, reach, cuts=(), kind=jnp.bfloat16):
    values = jax.random.normal(own_key, shape, jnp.float32) * width
    if len(cuts) > 0:
        values = shard_levels(own_key, shape, cuts, -0.22, 0.18) * values
    return jnp.clip(values, min=-reach, max=reach).astype(kind)


def setup_inputs(seed: int = 0) -> dict:
    splits = jax.random.split(jax.random.key(seed), 11)
    tokens = draw_tokens(jax.random.fold_in(splits[10], 71), 0)
    assigned_keys = jax.random.split(jax.random.fold_in(splits[1], 1), TOKENS // TOK_DEV)
    assigned_turns = jax.random.permutation(jax.random.fold_in(splits[1], 3), TOKENS // TOK_DEV)
    assigned = jax.vmap(lambda own, number: assign_block(jax.random.fold_in(splits[1], 2), own, number, TOK_DEV, EXPERTS, 1, CAP, 2))(assigned_keys, assigned_turns).reshape((TOKENS, 1))
    gate_prob = jnp.clip(0.2 + 0.8 * jax.random.uniform(splits[2], (TOKENS, 1), jnp.float32) ** shard_levels(splits[2], (TOKENS, 1), ((0, 32),), -0.2, 0.2), 0.2, 1.0)
    cotangent = draw_cotangent(jax.random.fold_in(splits[10], 71), 0)
    weight_in = gaussian(splits[4], (EXPERTS, D, FF), D ** -0.5, 0.21875, ((0, 4),))
    weight_out = gaussian(splits[5], (EXPERTS, FF, D), FF ** -0.5, 0.109375, ((0, 4),))
    moment_in = gaussian(splits[6], (EXPERTS, D, FF), 10.0, 60.0, ((0, 4), (1, 8)), jnp.float32)
    moment_out = gaussian(splits[7], (EXPERTS, FF, D), 10.0, 60.0, ((0, 4), (1, 8)), jnp.float32)
    second_in = jnp.clip(jnp.exp(math.log(1000.0) - 6.9077553 * jax.random.uniform(splits[8], (EXPERTS, D, FF), jnp.float32) ** shard_levels(splits[8], (EXPERTS, D, FF), ((0, 4), (1, 8)), -0.2, 0.2)), 1.0, 1000.0)
    second_out = jnp.clip(jnp.exp(math.log(1000.0) - 6.9077553 * jax.random.uniform(splits[9], (EXPERTS, FF, D), jnp.float32) ** shard_levels(splits[9], (EXPERTS, FF, D), ((0, 4), (1, 8)), -0.2, 0.2)), 1.0, 1000.0)
    return {"tokens": tokens, "assigned": assigned, "gate_prob": gate_prob, "cotangent": cotangent, "weight_in": weight_in, "weight_out": weight_out, "moment_in": moment_in, "moment_out": moment_out, "second_in": second_in, "second_out": second_out}


eps_adasum = 1e-06

def gelu_tanh(values):
    return jax.nn.gelu(values, approximate=True)

def adam_update(grad, weight, moment, second):
    new_moment = 0.9 * moment + 0.1 * grad
    new_second = 0.999 * second + 0.001 * grad * grad
    corr_one = 1.0 - 0.9 ** 10.0
    corr_two = 1.0 - 0.999 ** 10.0
    update = new_moment / corr_one / (jnp.sqrt(new_second / corr_two) + 1e-08)
    return (weight - 0.001 * update, new_moment, new_second)

def adasum(grad_in, grad_out):
    vectors = jnp.stack([grad_in.reshape(N_DP, -1), grad_out.reshape(N_DP, -1)], axis=1)
    count = N_DP
    for level in range(LEVELS):
        half_count = count // 2
        first = vectors[:half_count]
        second = vectors[half_count:count]
        cross = lax.optimization_barrier(jnp.sum(first * second, axis=(1, 2)))
        norm_first = lax.optimization_barrier(jnp.sum(first * first, axis=(1, 2)))
        norm_second = lax.optimization_barrier(jnp.sum(second * second, axis=(1, 2)))
        coef_first = 1.0 - cross / (2.0 * (norm_first + eps_adasum))
        coef_second = 1.0 - cross / (2.0 * (norm_second + eps_adasum))
        vectors = coef_first[:, None, None] * first + coef_second[:, None, None] * second
        count = half_count
    return vectors[0]

def reference(tokens, assigned, gate_prob, cotangent, weight_in, weight_out, moment_in, moment_out, second_in, second_out):
    f32 = jnp.float32
    bf16 = jnp.bfloat16
    blocks = N_DP * N_EXPERT
    expert_ids = assigned[:, 0].reshape(blocks, TOK_DEV)
    one_hot = (expert_ids[:, :, None] == jnp.arange(EXPERTS, dtype=jnp.int32)[None, None, :]).astype(jnp.int32)
    slot_index = lax.optimization_barrier(jnp.sum((jnp.cumsum(one_hot, axis=1) - one_hot) * one_hot, axis=2))
    slot_code = (expert_ids * CAP + slot_index).reshape(N_DP, N_EXPERT, TOK_DEV)
    scaled = (gate_prob * cotangent.astype(f32)).astype(bf16)
    token_blocks = tokens.reshape(N_DP, N_EXPERT, TOK_DEV, D)
    scaled_blocks = scaled.reshape(N_DP, N_EXPERT, TOK_DEV, D)
    buffer_rows = N_EXPERT * CAP

    def expert_step(expert):
        w_first = weight_in[expert]
        w_second = weight_out[expert]

        def replica(replica_index):
            codes = slot_code[replica_index]
            wanted = expert * CAP + jnp.arange(CAP, dtype=jnp.int32)
            table = (codes[:, None, :] == wanted[None, :, None]).astype(f32)
            dispatched = jnp.einsum('sct,std->scd', table, token_blocks[replica_index].astype(f32)).astype(bf16).reshape(buffer_rows, D)
            upstream = jnp.einsum('sct,std->scd', table, scaled_blocks[replica_index].astype(f32)).astype(bf16).reshape(buffer_rows, D)
            pre_act = jnp.dot(dispatched, w_first, preferred_element_type=f32)
            activated, gelu_back = jax.vjp(gelu_tanh, pre_act)
            hidden = activated.astype(bf16)
            expert_out = jnp.dot(hidden, w_second, preferred_element_type=f32).astype(bf16)
            grad_out = jnp.dot(hidden.T, upstream, preferred_element_type=f32)
            back_in = jnp.dot(upstream, w_second.T, preferred_element_type=f32)
            hidden_grad = gelu_back(back_in)[0].astype(bf16)
            grad_in = jnp.dot(dispatched.T, hidden_grad, preferred_element_type=f32)
            return (expert_out, grad_in, grad_out)
        outs_all, grads_in, grads_out = lax.map(replica, jnp.arange(N_DP, dtype=jnp.int32))
        total = adasum(grads_in, grads_out)
        new_w_first, new_m_first, new_v_first = adam_update(total[0].reshape(D, FF), w_first.astype(f32), moment_in[expert], second_in[expert])
        new_w_second, new_m_second, new_v_second = adam_update(total[1].reshape(FF, D), w_second.astype(f32), moment_out[expert], second_out[expert])
        return (outs_all, new_w_first, new_w_second, new_m_first, new_m_second, new_v_first, new_v_second)
    results = lax.map(expert_step, jnp.arange(EXPERTS, dtype=jnp.int32))
    outs_all = results[0]
    ids_three = expert_ids.reshape(N_DP, N_EXPERT, TOK_DEV)
    slots_three = slot_index.reshape(N_DP, N_EXPERT, TOK_DEV)
    replica_pos = jnp.arange(N_DP, dtype=jnp.int32)[:, None, None]
    source_pos = jnp.arange(N_EXPERT, dtype=jnp.int32)[None, :, None]
    picked = outs_all[ids_three, replica_pos, source_pos * CAP + slots_three]
    combined = (gate_prob.reshape(N_DP, N_EXPERT, TOK_DEV, 1) * picked.astype(f32)).astype(bf16).reshape(TOKENS, D)
    return (combined, results[1], results[2], results[3], results[4], results[5], results[6])
```

```python
import jax
import jax.numpy as jnp
from jax import lax
from jax.sharding import PartitionSpec as P

eps_adasum = 1e-06
f32 = jnp.float32
bf16 = jnp.bfloat16
f16 = jnp.float16


def swap(x, axis, offset):
    return lax.ppermute(x, axis, [(i, i ^ offset) for i in range(lax.axis_size(axis))])


def gelu_tanh(values):
    return jax.nn.gelu(values, approximate=True)


def adam_update(grad, weight, moment, second):
    new_moment = 0.9 * moment + 0.1 * grad
    new_second = 0.999 * second + 0.001 * grad * grad
    corr_one = 1.0 - 0.9**10.0
    corr_two = 1.0 - 0.999**10.0
    update = new_moment / corr_one / (jnp.sqrt(new_second / corr_two) + 1e-08)
    return (weight - 0.001 * update, new_moment, new_second)


def contract_rows(left, right):
    return lax.dot_general(
        left, right, (((0,), (0,)), ((), ())), preferred_element_type=f32
    )


def slot_table(assigned, expert, experts, capacity):
    expert_ids = assigned[:, 0]
    one_hot = (expert_ids[:, None] == jnp.arange(experts, dtype=jnp.int32)[None, :]).astype(
        jnp.int32
    )
    slot_index = jnp.sum((jnp.cumsum(one_hot, axis=0) - one_hot) * one_hot, axis=1)
    slot_code = (expert_ids ^ expert) * capacity + slot_index
    rows = experts * capacity
    return (jnp.arange(rows, dtype=jnp.int32)[:, None] == slot_code[None, :]).astype(bf16)


def exchange_blocks(blocks):
    return [blocks[0]] + [swap(blocks[j], "expert", j) for j in range(1, len(blocks))]


def dispatch(table, rows, experts):
    capacity = table.shape[0] // experts
    sent = jnp.dot(table, rows, preferred_element_type=f32).astype(bf16)
    blocks = [sent[j * capacity : (j + 1) * capacity] for j in range(experts)]
    return jnp.concatenate(exchange_blocks(blocks), axis=0)


def xor_both(gram, bit):
    count = gram.shape[0]
    split = gram.reshape(count // (2 * bit), 2, bit, count // (2 * bit), 2, bit)
    return split[:, ::-1, :, :, ::-1, :].reshape(count, count)


def xor_one(vector, bit):
    count = vector.shape[0]
    return vector.reshape(count // (2 * bit), 2, bit)[:, ::-1, :].reshape(count)


def body(
    tokens,
    assigned,
    gate_prob,
    cotangent,
    weight_in,
    weight_out,
    moment_in,
    moment_out,
    second_in,
    second_out,
):
    experts = lax.axis_size("expert")
    replicas = lax.axis_size("dp")
    top = replicas // 2
    self_index = lax.axis_index("dp")
    expert = lax.axis_index("expert")
    half = self_index // top
    member = self_index % top
    tok_rows, width = tokens.shape
    hidden_width = weight_in.shape[2]
    capacity = 2 * tok_rows // experts
    rows_first = width // replicas
    rows_second = hidden_width // replicas
    w_first = weight_in[0]
    w_second = weight_out[0]

    scaled = (gate_prob * cotangent.astype(f32)).astype(bf16)
    far_assigned = swap(assigned, "dp", top)
    far_tokens = swap(tokens, "dp", top)
    far_scaled = swap(scaled, "dp", top)

    table = slot_table(assigned, expert, experts, capacity)
    inputs = dispatch(table, tokens, experts)
    upstream = dispatch(table, scaled, experts)

    def forward(rows):
        pre_act = jnp.dot(rows, w_first, preferred_element_type=f32)
        activated, gelu_back = jax.vjp(gelu_tanh, pre_act)
        return activated.astype(bf16), gelu_back

    def half_grads(rows, hidden, gelu_back, ups):
        back_in = lax.dot_general(
            ups, w_second, (((1,), (1,)), ((), ())), preferred_element_type=f32
        )
        hidden_grad = gelu_back(back_in)[0].astype(bf16)
        rows_half = lax.dynamic_slice_in_dim(rows, half * (width // 2), width // 2, 1)
        hidden_half = lax.dynamic_slice_in_dim(
            hidden, half * (hidden_width // 2), hidden_width // 2, 1
        )
        return contract_rows(rows_half, hidden_grad), contract_rows(hidden_half, ups)

    hidden, gelu_back = forward(inputs)
    expert_out = jnp.dot(hidden, w_second, preferred_element_type=f32).astype(bf16)
    own_in, own_out = half_grads(inputs, hidden, gelu_back, upstream)

    far_table = slot_table(far_assigned, expert, experts, capacity)
    far_inputs = dispatch(far_table, far_tokens, experts)
    far_upstream = dispatch(far_table, far_scaled, experts)
    far_hidden, far_gelu_back = forward(far_inputs)
    far_in, far_out = half_grads(far_inputs, far_hidden, far_gelu_back, far_upstream)

    mine = jnp.stack(
        [
            jnp.sum(own_in * far_in) + jnp.sum(own_out * far_out),
            jnp.sum(own_in * own_in) + jnp.sum(own_out * own_out),
            jnp.sum(far_in * far_in) + jnp.sum(far_out * far_out),
        ]
    )
    theirs = swap(mine, "dp", top)
    cross = mine[0] + theirs[0]
    norm_own = mine[1] + theirs[2]
    norm_far = mine[2] + theirs[1]
    coef_own = 1.0 - cross / (2.0 * (norm_own + eps_adasum))
    coef_far = 1.0 - cross / (2.0 * (norm_far + eps_adasum))
    weighted = coef_own * coef_own * norm_own + coef_far * coef_far * norm_far
    norm = jnp.maximum(weighted + 2.0 * coef_own * coef_far * cross, 1e-5 * weighted)
    scale = 16384.0 * lax.rsqrt(jnp.maximum(norm, 1e-12))
    weight_own = coef_own * scale
    weight_far = coef_far * scale

    def quarter(other):
        place = member ^ other
        first = weight_own * lax.dynamic_slice_in_dim(
            own_in, place * rows_first, rows_first, 0
        ) + weight_far * lax.dynamic_slice_in_dim(far_in, place * rows_first, rows_first, 0)
        second = weight_own * lax.dynamic_slice_in_dim(
            own_out, place * rows_second, rows_second, 0
        ) + weight_far * lax.dynamic_slice_in_dim(far_out, place * rows_second, rows_second, 0)
        return first, second

    parts = [quarter(0)]
    for other in range(1, top):
        first, second = quarter(other)
        parts.append(
            (
                swap(first.astype(f16), "dp", other).astype(f32),
                swap(second.astype(f16), "dp", other).astype(f32),
            )
        )

    gram = {}
    for j in range(top):
        for k in range(j, top):
            gram[j, k] = jnp.sum(parts[j][0] * parts[k][0]) + jnp.sum(parts[j][1] * parts[k][1])
            gram[k, j] = gram[j, k]
    sums = jnp.stack([jnp.stack([gram[j, k] for k in range(top)]) for j in range(top)])
    scales = jnp.where(jnp.arange(top) == 0, scale, 0.0)
    bit = 1
    while bit < replicas:
        packed = jnp.concatenate([sums.reshape(-1), scales])
        packed = swap(packed, "dp", bit)
        other_sums = packed[: top * top].reshape(top, top)
        if bit < top:
            sums = sums + xor_both(other_sums, bit)
            scales = scales + xor_one(packed[top * top :], bit)
        else:
            sums = sums + other_sums
        bit *= 2
    unscale = 1.0 / scales
    sums = sums * unscale[:, None] * unscale[None, :]
    vectors = [(parts[j][0] * unscale[j], parts[j][1] * unscale[j]) for j in range(top)]
    count = top
    while count > 1:
        bit = count // 2
        low, high = sums[:bit, :bit], sums[bit:, bit:]
        mix = sums[:bit, bit:]
        norm_low = jnp.maximum(jnp.diagonal(low), 0.0)
        norm_high = jnp.maximum(jnp.diagonal(high), 0.0)
        limit = jnp.sqrt(norm_low) * jnp.sqrt(norm_high)
        product = jnp.clip(jnp.diagonal(mix), -limit, limit)
        coef_low = 1.0 - product / (2.0 * (norm_low + eps_adasum))
        coef_high = 1.0 - product / (2.0 * (norm_high + eps_adasum))
        vectors = [
            tuple(
                coef_low[j] * vectors[j][n] + coef_high[j] * vectors[j + bit][n] for n in range(2)
            )
            for j in range(bit)
        ]
        crossed = coef_low[:, None] * coef_high[None, :] * mix
        sums = (
            coef_low[:, None] * coef_low[None, :] * low
            + coef_high[:, None] * coef_high[None, :] * high
            + crossed
            + crossed.T
        )
        count = bit
    seg_first, seg_second = vectors[0]

    own_first = lax.dynamic_slice_in_dim(w_first, self_index * rows_first, rows_first, 0).astype(
        f32
    )
    own_second = lax.dynamic_slice_in_dim(
        w_second, self_index * rows_second, rows_second, 0
    ).astype(f32)
    new_w_first, new_m_first, new_v_first = adam_update(
        seg_first, own_first, moment_in[0], second_in[0]
    )
    new_w_second, new_m_second, new_v_second = adam_update(
        seg_second, own_second, moment_out[0], second_out[0]
    )

    returned = exchange_blocks(
        [expert_out[j * capacity : (j + 1) * capacity] for j in range(experts)]
    )
    picked = contract_rows(table, jnp.concatenate(returned, axis=0))
    combined = (gate_prob * picked).astype(bf16)
    return (
        combined,
        new_w_first[None],
        new_w_second[None],
        new_m_first[None],
        new_m_second[None],
        new_v_first[None],
        new_v_second[None],
    )


def solution(mesh):
    row_spec = P(("dp", "expert"), None)
    owner_spec = P("expert", "dp", None)
    return jax.shard_map(
        body,
        mesh=mesh,
        in_specs=(row_spec,) * 4 + (P("expert", None, None),) * 2 + (owner_spec,) * 4,
        out_specs=(row_spec,) + (owner_spec,) * 6,
        check_vma=False,
    )
```

```python
import functools

import jax
import jax.numpy as jnp
from jax import lax
from jax.experimental import pallas as pl
from jax.experimental.pallas import tpu as pltpu
from jax.sharding import PartitionSpec as P

eps_adasum = 1e-06
f32 = jnp.float32
bf16 = jnp.bfloat16
f16 = jnp.float16
VMEM_LIMIT = 48 << 20


def swap(x, axis, offset):
    return lax.ppermute(x, axis, [(i, i ^ offset) for i in range(lax.axis_size(axis))])


def gelu_and_slope(values):
    root = 0.7978845608028654
    square = values * values
    tanh = jnp.tanh(values * (root + (root * 0.044715) * square))
    cdf = 0.5 + 0.5 * tanh
    slope = cdf + (0.5 * values) * (1.0 - tanh * tanh) * (root + (3.0 * root * 0.044715) * square)
    return values * cdf, slope


def adam_update(grad, weight, moment, second):
    new_moment = 0.9 * moment + 0.1 * grad
    new_second = 0.999 * second + 0.001 * grad * grad
    corr_one = 1.0 - 0.9**10.0
    corr_two = 1.0 - 0.999**10.0
    update = new_moment / corr_one / (jnp.sqrt(new_second / corr_two) + 1e-08)
    return (weight - 0.001 * update, new_moment, new_second)


def contract_rows(left, right):
    return lax.dot_general(
        left, right, (((0,), (0,)), ((), ())), preferred_element_type=f32
    )


def slot_table(assigned, expert, experts, capacity):
    expert_ids = assigned[:, 0]
    one_hot = (expert_ids[:, None] == jnp.arange(experts, dtype=jnp.int32)[None, :]).astype(
        jnp.int32
    )
    slot_index = jnp.sum((jnp.cumsum(one_hot, axis=0) - one_hot) * one_hot, axis=1)
    slot_code = (expert_ids ^ expert) * capacity + slot_index
    rows = experts * capacity
    return (jnp.arange(rows, dtype=jnp.int32)[:, None] == slot_code[None, :]).astype(bf16)


def exchange_blocks(blocks):
    return [blocks[0]] + [swap(blocks[j], "expert", j) for j in range(1, len(blocks))]


def dispatch(table, rows, experts):
    capacity = table.shape[0] // experts
    sent = jnp.dot(table, rows, preferred_element_type=f32).astype(bf16)
    blocks = [sent[j * capacity : (j + 1) * capacity] for j in range(experts)]
    return jnp.concatenate(exchange_blocks(blocks), axis=0)


def fold(values):
    rows = values.reshape(values.shape[0] // 8, 8, values.shape[1]).sum(0)
    spare = -rows.shape[1] % 128
    if spare:
        rows = jnp.concatenate([rows, jnp.zeros((8, spare), f32)], axis=1)
    return sum(rows[:, k * 128 : (k + 1) * 128] for k in range(rows.shape[1] // 128))


def expert_kernel(half_ref, x_ref, u_ref, w1_ref, w2_ref, *rest, steps, own):
    if own:
        out_ref, gi_ref, go_ref, xt_ref, ut_ref, acc_ref = rest
    else:
        own_gi_ref, own_go_ref, gi_ref, go_ref, stat_ref, xt_ref, ut_ref, acc_ref = rest
    step = pl.program_id(0)
    half_width = xt_ref.shape[0]

    @pl.when(step == 0)
    def _():
        start = pl.multiple_of(half_ref[0] * half_width, half_width)
        xt_ref[...] = x_ref[:, pl.ds(start, half_width)].T
        ut_ref[...] = u_ref[...].T

    pre = jnp.dot(x_ref[...], w1_ref[...], preferred_element_type=f32)
    back = lax.dot_general(
        u_ref[...], w2_ref[...], (((1,), (1,)), ((), ())), preferred_element_type=f32
    )
    act, slope = gelu_and_slope(pre)
    hidden = act.astype(bf16)
    hidden_grad = (slope * back).astype(bf16)
    gi_ref[...] = jnp.dot(xt_ref[...], hidden_grad, preferred_element_type=f32)

    @pl.when(step < steps // 2)
    def _():
        go_ref[...] = jnp.dot(ut_ref[...], hidden, preferred_element_type=f32)

    if own:
        product = jnp.dot(hidden, w2_ref[...], preferred_element_type=f32)

        @pl.when(step == 0)
        def _():
            acc_ref[...] = product

        @pl.when(step > 0)
        def _():
            acc_ref[...] += product

        @pl.when(step == steps - 1)
        def _():
            out_ref[...] = acc_ref[...].astype(bf16)

    else:

        def add(mine, far):
            acc_ref[0] += fold(mine * far)
            acc_ref[1] += fold(mine * mine)
            acc_ref[2] += fold(far * far)

        @pl.when(step == 0)
        def _():
            acc_ref[...] = jnp.zeros_like(acc_ref)

        add(own_gi_ref[...], gi_ref[...])

        @pl.when(step < steps // 2)
        def _():
            add(own_go_ref[...], go_ref[...])

        @pl.when(step == steps - 1)
        def _():
            row = lax.broadcasted_iota(jnp.int32, (8, 128), 0)
            stats = jnp.zeros((8, 128), f32)
            for k in range(3):
                stats = jnp.where(row == k, jnp.sum(acc_ref[k]), stats)
            stat_ref[...] = stats


def expert_call(half, x, u, w1, w2, previous):
    rows, width = x.shape
    hidden_width = w1.shape[1]
    steps = 6
    block = hidden_width // steps
    own = previous is None

    def column(i, h):
        return (0, (i + h[0] * (steps // 2)) % steps)

    def row(i, h):
        return ((i + h[0] * (steps // 2)) % steps, 0)

    def held(i, h):
        return (0, jnp.minimum(i, steps // 2 - 1))

    def whole(i, h):
        return (0, 0)

    one = pl.Buffered(1)
    in_specs = [
        pl.BlockSpec((rows, width), whole, pipeline_mode=one),
        pl.BlockSpec((rows, width), whole, pipeline_mode=one),
        pl.BlockSpec((width, block), column),
        pl.BlockSpec((block, width), row),
    ]
    grad_specs = [pl.BlockSpec((width // 2, block), column), pl.BlockSpec((width, block), held)]
    grad_shapes = [
        jax.ShapeDtypeStruct((width // 2, hidden_width), f32),
        jax.ShapeDtypeStruct((width, hidden_width // 2), f32),
    ]
    scratch = [pltpu.VMEM((width // 2, rows), bf16), pltpu.VMEM((width, rows), bf16)]
    args = [x, u, w1, w2]
    if own:
        out_specs = [pl.BlockSpec((rows, width), whole)] + grad_specs
        out_shape = [jax.ShapeDtypeStruct((rows, width), bf16)] + grad_shapes
        scratch.append(pltpu.VMEM((rows, width), f32))
    else:
        in_specs += grad_specs
        args += list(previous)
        out_specs = grad_specs + [pl.BlockSpec((8, 128), whole)]
        out_shape = grad_shapes + [jax.ShapeDtypeStruct((8, 128), f32)]
        scratch.append(pltpu.VMEM((3, 8, 128), f32))
    return pl.pallas_call(
        functools.partial(expert_kernel, steps=steps, own=own),
        grid_spec=pltpu.PrefetchScalarGridSpec(
            num_scalar_prefetch=1,
            grid=(steps,),
            in_specs=in_specs,
            out_specs=out_specs,
            scratch_shapes=scratch,
        ),
        out_shape=out_shape,
        compiler_params=pltpu.CompilerParams(vmem_limit_bytes=VMEM_LIMIT),
        cost_estimate=pl.CostEstimate(
            flops=(8 if own else 6) * rows * width * hidden_width,
            bytes_accessed=30 << 20,
            transcendentals=rows * hidden_width,
        ),
    )(half, *args)


def gram_kernel(info_ref, scale_ref, *refs, count):
    firsts, seconds, out_ref, acc_ref = refs[:count], refs[count : 2 * count], refs[-2], refs[-1]
    step = pl.program_id(0)
    pairs = [(j, k) for j in range(count) for k in range(j, count)]

    @pl.when(step == 0)
    def _():
        acc_ref[...] = jnp.zeros_like(acc_ref)

    for group in (firsts, seconds):
        values = [ref[...] for ref in group]
        for n, (j, k) in enumerate(pairs):
            acc_ref[n] += fold(values[j] * values[k])

    @pl.when(step == pl.num_programs(0) - 1)
    def _():
        member = info_ref[0]
        row = lax.broadcasted_iota(jnp.int32, out_ref.shape, 0)
        lane = lax.broadcasted_iota(jnp.int32, out_ref.shape, 1)
        table = jnp.where((row == member) & (lane == count), 0.5 * scale_ref[...], 0.0)
        for n, (j, k) in enumerate(pairs):
            total = jnp.sum(acc_ref[n])
            a, b = member ^ j, member ^ k
            here = ((row == a) & (lane == b)) | ((row == b) & (lane == a))
            table = jnp.where(here, total, table)
        out_ref[...] = table


def gram_call(member, scale, firsts, seconds):
    count = len(firsts)
    steps = 3
    first_block = (firsts[0].shape[0], firsts[0].shape[1] // steps)
    second_block = (seconds[0].shape[0] // steps, seconds[0].shape[1])
    rows = 8 * -(-count // 8)
    pairs = count * (count + 1) // 2
    return pl.pallas_call(
        functools.partial(gram_kernel, count=count),
        grid_spec=pltpu.PrefetchScalarGridSpec(
            num_scalar_prefetch=1,
            grid=(steps,),
            in_specs=[pl.BlockSpec((1, 1), lambda i, h: (0, 0))]
            + [pl.BlockSpec(first_block, lambda i, h: (0, i))] * count
            + [pl.BlockSpec(second_block, lambda i, h: (i, 0))] * count,
            out_specs=pl.BlockSpec((rows, 128), lambda i, h: (0, 0)),
            scratch_shapes=[pltpu.VMEM((pairs, 8, 128), f32)],
        ),
        out_shape=jax.ShapeDtypeStruct((rows, 128), f32),
        compiler_params=pltpu.CompilerParams(vmem_limit_bytes=VMEM_LIMIT),
    )(member, scale, *firsts, *seconds)


def tree_weights(table_ref, member, count):
    table = table_ref[...]
    row = lax.broadcasted_iota(jnp.int32, table.shape, 0)
    lane = lax.broadcasted_iota(jnp.int32, table.shape, 1)

    def entry(a, b):
        picked = jnp.where((row == a) & (lane == b), table, 0.0)
        return jnp.sum(jnp.sum(picked, axis=1, keepdims=True), axis=0, keepdims=True)

    unscale = [1.0 / entry(member ^ j, count) for j in range(count)]
    gram = {}
    for j in range(count):
        for k in range(j, count):
            gram[j, k] = entry(member ^ j, member ^ k) * unscale[j] * unscale[k]
    factors = {}
    left = count
    while left > 1:
        bit = left // 2
        low, high = [], []
        for j in range(bit):
            norm_low = jnp.maximum(gram[j, j], 0.0)
            norm_high = jnp.maximum(gram[j + bit, j + bit], 0.0)
            limit = jnp.sqrt(norm_low) * jnp.sqrt(norm_high)
            product = jnp.clip(gram[j, j + bit], -limit, limit)
            low.append(1.0 - product / (2.0 * (norm_low + eps_adasum)))
            high.append(1.0 - product / (2.0 * (norm_high + eps_adasum)))
        factors[bit] = (low, high)
        gram = {
            (j, k): low[j] * low[k] * gram[j, k]
            + high[j] * high[k] * gram[j + bit, k + bit]
            + (low[j] * high[k] * gram[j, k + bit] + low[k] * high[j] * gram[k, j + bit])
            for j in range(bit)
            for k in range(j, bit)
        }
        left = bit
    return unscale, factors


def update_kernel(info_ref, table_ref, *refs, count):
    firsts, seconds = refs[:count], refs[count : 2 * count]
    w1_ref, w2_ref, m1_ref, m2_ref, v1_ref, v2_ref = refs[2 * count : 2 * count + 6]
    outs = refs[2 * count + 6 :]
    unscale, factors = tree_weights(table_ref, info_ref[0], count)

    def combine(group):
        values = [group[j][...] * unscale[j] for j in range(count)]
        left = count
        while left > 1:
            left //= 2
            low, high = factors[left]
            values = [low[j] * values[j] + high[j] * values[j + left] for j in range(left)]
        return values[0]

    grad = combine(firsts)
    new = adam_update(grad, w1_ref[0].astype(f32), m1_ref[0], v1_ref[0])
    for n in range(3):
        outs[2 * n][0] = new[n]
    grad = combine(seconds).T
    new = adam_update(grad, w2_ref[0].astype(f32), m2_ref[0], v2_ref[0])
    for n in range(3):
        outs[2 * n + 1][0] = new[n]


def update_call(info, table, firsts, seconds, w1, w2, m1, m2, v1, v2):
    count = len(firsts)
    steps = 3
    rows_first, hidden_width = firsts[0].shape
    width, rows_second = seconds[0].shape
    first_block = (rows_first, hidden_width // steps)
    second_block = (width // steps, rows_second)
    first_own = pl.BlockSpec((1,) + first_block, lambda i, h: (0, 0, i))
    second_own = pl.BlockSpec((1, rows_second, width // steps), lambda i, h: (0, 0, i))
    return pl.pallas_call(
        functools.partial(update_kernel, count=count),
        grid_spec=pltpu.PrefetchScalarGridSpec(
            num_scalar_prefetch=1,
            grid=(steps,),
            in_specs=[pl.BlockSpec(table.shape, lambda i, h: (0, 0))]
            + [pl.BlockSpec(first_block, lambda i, h: (0, i))] * count
            + [pl.BlockSpec(second_block, lambda i, h: (i, 0))] * count
            + [
                pl.BlockSpec((1,) + first_block, lambda i, h: (0, h[1], i)),
                pl.BlockSpec((1, rows_second, width // steps), lambda i, h: (0, h[1], i)),
            ]
            + [first_own, second_own] * 2,
            out_specs=[first_own, second_own] * 3,
        ),
        out_shape=[
            jax.ShapeDtypeStruct((1, rows_first, hidden_width), f32),
            jax.ShapeDtypeStruct((1, rows_second, width), f32),
        ]
        * 3,
        compiler_params=pltpu.CompilerParams(vmem_limit_bytes=VMEM_LIMIT),
    )(info, table, *firsts, *seconds, w1, w2, m1, m2, v1, v2)


def body(
    tokens,
    assigned,
    gate_prob,
    cotangent,
    weight_in,
    weight_out,
    moment_in,
    moment_out,
    second_in,
    second_out,
):
    experts = lax.axis_size("expert")
    replicas = lax.axis_size("dp")
    top = replicas // 2
    self_index = lax.axis_index("dp")
    expert = lax.axis_index("expert")
    half = self_index // top
    member = self_index % top
    tok_rows, width = tokens.shape
    hidden_width = weight_in.shape[2]
    capacity = 2 * tok_rows // experts
    rows_first = width // replicas
    rows_second = hidden_width // replicas
    w_first = weight_in[0]
    w_second = weight_out[0]
    half_info = half.astype(jnp.int32).reshape(1)
    info = jnp.stack([member, self_index]).astype(jnp.int32)

    scaled = (gate_prob * cotangent.astype(f32)).astype(bf16)
    far_assigned = swap(assigned, "dp", top)
    far_tokens = swap(tokens, "dp", top)
    far_scaled = swap(scaled, "dp", top)

    table = slot_table(assigned, expert, experts, capacity)
    inputs = dispatch(table, tokens, experts)
    upstream = dispatch(table, scaled, experts)
    expert_out, own_in, own_out = expert_call(
        half_info, inputs, upstream, w_first, w_second, None
    )

    far_table = slot_table(far_assigned, expert, experts, capacity)
    far_inputs = dispatch(far_table, far_tokens, experts)
    far_upstream = dispatch(far_table, far_scaled, experts)
    far_in, far_out, mine = expert_call(
        half_info, far_inputs, far_upstream, w_first, w_second, (own_in, own_out)
    )

    theirs = swap(mine, "dp", top)
    cross = mine[0, 0] + theirs[0, 0]
    norm_own = mine[1, 0] + theirs[2, 0]
    norm_far = mine[2, 0] + theirs[1, 0]
    coef_own = 1.0 - cross / (2.0 * (norm_own + eps_adasum))
    coef_far = 1.0 - cross / (2.0 * (norm_far + eps_adasum))
    weighted = coef_own * coef_own * norm_own + coef_far * coef_far * norm_far
    norm = jnp.maximum(weighted + 2.0 * coef_own * coef_far * cross, 1e-5 * weighted)
    scale = 16384.0 * lax.rsqrt(jnp.maximum(norm, 1e-12))
    weight_own = coef_own * scale
    weight_far = coef_far * scale

    def quarter(other):
        place = member ^ other

        def part(own, far, size, axis):
            own, far = (
                lax.dynamic_slice_in_dim(x, place * size, size, axis) for x in (own, far)
            )
            return weight_own * own + weight_far * far

        return part(own_in, far_in, rows_first, 0), part(own_out, far_out, rows_second, 1)

    firsts, seconds = [], []
    for other in range(top):
        first, second = quarter(other)
        if other:
            first = swap(first.astype(f16), "dp", other).astype(f32)
            second = swap(second.astype(f16), "dp", other).astype(f32)
        firsts.append(first)
        seconds.append(second)

    products = gram_call(info, scale.reshape(1, 1), firsts, seconds)
    bit = 1
    while bit < replicas:
        products = products + swap(products, "dp", bit)
        bit *= 2
    new = update_call(
        info,
        products,
        firsts,
        seconds,
        weight_in,
        weight_out,
        moment_in,
        moment_out,
        second_in,
        second_out,
    )

    returned = exchange_blocks(
        [expert_out[j * capacity : (j + 1) * capacity] for j in range(experts)]
    )
    picked = contract_rows(table, jnp.concatenate(returned, axis=0))
    combined = (gate_prob * picked).astype(bf16)
    return (combined, *new)


def solution(mesh):
    row_spec = P(("dp", "expert"), None)
    owner_spec = P("expert", "dp", None)
    return jax.shard_map(
        body,
        mesh=mesh,
        in_specs=(row_spec,) * 4 + (P("expert", None, None),) * 2 + (owner_spec,) * 4,
        out_specs=(row_spec,) + (owner_spec,) * 6,
        check_vma=False,
    )
```

```python
import functools

import jax
import jax.numpy as jnp
from jax import lax
from jax.experimental import pallas as pl
from jax.experimental.pallas import tpu as pltpu
from jax.sharding import PartitionSpec as P

eps_adasum = 1e-06
f32 = jnp.float32
bf16 = jnp.bfloat16
f16 = jnp.float16
VMEM_LIMIT = 48 << 20
GRAM_LIMIT = 8 << 20
UPDATE_LIMIT = 20 << 20
COST = 1 << 10
COST = 1 << 10
TOKEN_PIECES = 1
SCALED_PIECES = 1
CHAIN = False


def swap(x, axis, offset):
    return lax.ppermute(x, axis, [(i, i ^ offset) for i in range(lax.axis_size(axis))])


def gelu_and_slope(values):
    root = 0.7978845608028654
    square = values * values
    tanh = jnp.tanh(values * (root + (root * 0.044715) * square))
    cdf = 0.5 + 0.5 * tanh
    slope = cdf + (0.5 * values) * (1.0 - tanh * tanh) * (root + (3.0 * root * 0.044715) * square)
    return values * cdf, slope


def adam_update(grad, weight, moment, second):
    new_moment = 0.9 * moment + 0.1 * grad
    new_second = 0.999 * second + 0.001 * grad * grad
    corr_one = 1.0 - 0.9**10.0
    corr_two = 1.0 - 0.999**10.0
    update = new_moment / corr_one / (jnp.sqrt(new_second / corr_two) + 1e-08)
    return (weight - 0.001 * update, new_moment, new_second)


def contract_rows(left, right):
    return lax.dot_general(
        left, right, (((0,), (0,)), ((), ())), preferred_element_type=f32
    )


def slot_table(assigned, expert, experts, capacity):
    expert_ids = assigned[:, 0]
    one_hot = (expert_ids[:, None] == jnp.arange(experts, dtype=jnp.int32)[None, :]).astype(
        jnp.int32
    )
    slot_index = jnp.sum((jnp.cumsum(one_hot, axis=0) - one_hot) * one_hot, axis=1)
    slot_code = (expert_ids ^ expert) * capacity + slot_index
    rows = experts * capacity
    return (jnp.arange(rows, dtype=jnp.int32)[:, None] == slot_code[None, :]).astype(bf16)


def exchange_blocks(blocks):
    return [blocks[0]] + [swap(blocks[j], "expert", j) for j in range(1, len(blocks))]


def place_rows(table, rows, experts):
    capacity = table.shape[0] // experts
    sent = jnp.dot(table, rows, preferred_element_type=f32).astype(bf16)
    return [sent[j * capacity : (j + 1) * capacity] for j in range(experts)]


def dispatch(table, rows, experts):
    placed = place_rows(table, rows, experts)
    return jnp.concatenate(exchange_blocks(placed), axis=0), placed


def fold(values):
    rows = values.reshape(values.shape[0] // 8, 8, values.shape[1]).sum(0)
    spare = -rows.shape[1] % 128
    if spare:
        rows = jnp.concatenate([rows, jnp.zeros((8, spare), f32)], axis=1)
    return sum(rows[:, k * 128 : (k + 1) * 128] for k in range(rows.shape[1] // 128))


def expert_kernel(info_ref, x_ref, u_ref, w1_ref, w2_ref, *rest, steps, kind):
    if kind == "first":
        gi_ref, go_ref, sum_ref, xt_ref, ut_ref = rest
    elif kind == "second":
        before_ref, _, gi_ref, out_ref, xt_ref, sum_ref = rest
    else:
        own_gi_ref, own_go_ref, gi_ref, go_ref, stat_ref, xt_ref, ut_ref, acc_ref = rest
    step = pl.program_id(0)
    half_width = xt_ref.shape[0]

    @pl.when(step == 0)
    def _():
        start = pl.multiple_of(info_ref[2] * half_width, half_width)
        xt_ref[...] = x_ref[:, pl.ds(start, half_width)].T
        if kind != "second":
            ut_ref[...] = u_ref[...].T

    pre = jnp.dot(x_ref[...], w1_ref[...], preferred_element_type=f32)
    back = lax.dot_general(
        u_ref[...], w2_ref[...], (((1,), (1,)), ((), ())), preferred_element_type=f32
    )
    act, slope = gelu_and_slope(pre)
    hidden = act.astype(bf16)
    hidden_grad = (slope * back).astype(bf16)
    gi_ref[...] = jnp.dot(xt_ref[...], hidden_grad, preferred_element_type=f32)

    if kind == "first":
        go_ref[...] = jnp.dot(ut_ref[...], hidden, preferred_element_type=f32)
    elif kind == "far":

        @pl.when(step < steps // 2)
        def _():
            go_ref[...] = jnp.dot(ut_ref[...], hidden, preferred_element_type=f32)

    if kind == "far":

        def add(mine, far):
            acc_ref[0] += fold(mine * far)
            acc_ref[1] += fold(mine * mine)
            acc_ref[2] += fold(far * far)

        @pl.when(step == 0)
        def _():
            acc_ref[...] = jnp.zeros_like(acc_ref)

        add(own_gi_ref[...], gi_ref[...])

        @pl.when(step < steps // 2)
        def _():
            add(own_go_ref[...], go_ref[...])

        @pl.when(step == steps - 1)
        def _():
            row = lax.broadcasted_iota(jnp.int32, (8, 128), 0)
            stats = jnp.zeros((8, 128), f32)
            for k in range(3):
                stats = jnp.where(row == k, jnp.sum(acc_ref[k]), stats)
            stat_ref[...] = stats

    else:
        product = jnp.dot(hidden, w2_ref[...], preferred_element_type=f32)

        @pl.when(step == 0)
        def _():
            sum_ref[...] = product if kind == "first" else before_ref[...] + product

        @pl.when(step > 0)
        def _():
            sum_ref[...] += product

        if kind == "second":

            @pl.when(step == steps // 2 - 1)
            def _():
                out_ref[...] = sum_ref[...].astype(bf16)


def expert_call(kind, info, x, u, w1, w2, *previous):
    rows, width = x.shape
    hidden_width = w1.shape[1]
    steps = 6
    block = hidden_width // steps
    shift = steps // 2 if kind == "second" else 0

    def column(i, h):
        return (0, (i + shift + h[2] * (steps // 2)) % steps)

    def row(i, h):
        return ((i + shift + h[2] * (steps // 2)) % steps, 0)

    def held(i, h):
        return (0, jnp.minimum(i, steps // 2 - 1))

    def whole(i, h):
        return (0, 0)

    one = pl.Buffered(1)
    whole_spec = pl.BlockSpec((rows, width), whole, pipeline_mode=one)
    in_specs = [
        whole_spec,
        whole_spec,
        pl.BlockSpec((width, block), column),
        pl.BlockSpec((block, width), row),
    ]
    gi_spec = pl.BlockSpec((width // 2, block), column)
    go_spec = pl.BlockSpec((width, block), held)
    gi_shape = jax.ShapeDtypeStruct((width // 2, hidden_width), f32)
    go_shape = jax.ShapeDtypeStruct((width, hidden_width // 2), f32)
    sum_shape = jax.ShapeDtypeStruct((rows, width), f32)
    xt = pltpu.VMEM((width // 2, rows), bf16)
    ut = pltpu.VMEM((width, rows), bf16)
    aliases = {}
    if kind == "first":
        out_specs = [gi_spec, go_spec, whole_spec]
        out_shape = [gi_shape, go_shape, sum_shape]
        scratch = [xt, ut]
    elif kind == "second":
        in_specs += [whole_spec, pl.BlockSpec(memory_space=pl.ANY)]
        out_specs = [gi_spec, whole_spec]
        out_shape = [gi_shape, jax.ShapeDtypeStruct((rows, width), bf16)]
        scratch = [xt, pltpu.VMEM((rows, width), f32)]
        aliases = {6: 0}
    else:
        in_specs += [gi_spec, go_spec]
        out_specs = [gi_spec, go_spec, pl.BlockSpec((8, 128), whole)]
        out_shape = [gi_shape, go_shape, jax.ShapeDtypeStruct((8, 128), f32)]
        scratch = [xt, ut, pltpu.VMEM((3, 8, 128), f32)]
    return pl.pallas_call(
        functools.partial(expert_kernel, steps=steps, kind=kind),
        grid_spec=pltpu.PrefetchScalarGridSpec(
            num_scalar_prefetch=1,
            grid=(steps if kind == "far" else steps // 2,),
            in_specs=in_specs,
            out_specs=out_specs,
            scratch_shapes=scratch,
        ),
        out_shape=out_shape,
        input_output_aliases=aliases,
        compiler_params=pltpu.CompilerParams(vmem_limit_bytes=VMEM_LIMIT),
        cost_estimate=pl.CostEstimate(
            flops=COST, bytes_accessed=COST, transcendentals=0
        ),
    )(info, x, u, w1, w2, *previous)


def gram_kernel(info_ref, before_ref, *refs, count, opening):
    group, out_ref, acc_ref = refs[:count], refs[-2], refs[-1]
    step = pl.program_id(0)
    pairs = [(j, k) for j in range(count) for k in range(j, count)]

    @pl.when(step == 0)
    def _():
        acc_ref[...] = jnp.zeros_like(acc_ref)

    values = [ref[...] for ref in group]
    for n, (j, k) in enumerate(pairs):
        acc_ref[n] += fold(values[j] * values[k])

    @pl.when(step == pl.num_programs(0) - 1)
    def _():
        member = info_ref[0]
        row = lax.broadcasted_iota(jnp.int32, out_ref.shape, 0)
        lane = lax.broadcasted_iota(jnp.int32, out_ref.shape, 1)
        table = jnp.zeros(out_ref.shape, f32)
        if opening:
            table = jnp.where((row == member) & (lane == count), 0.5 * before_ref[...], 0.0)
        for n, (j, k) in enumerate(pairs):
            total = jnp.sum(acc_ref[n])
            a, b = member ^ j, member ^ k
            here = ((row == a) & (lane == b)) | ((row == b) & (lane == a))
            table = jnp.where(here, total, table)
        out_ref[...] = table if opening else table + before_ref[...]


def gram_call(info, before, group, opening):
    count = len(group)
    steps = 3
    if opening:
        block, place = (group[0].shape[0], group[0].shape[1] // steps), lambda i, h: (0, i)
    else:
        block, place = (group[0].shape[0] // steps, group[0].shape[1]), lambda i, h: (i, 0)
    rows = 8 * -(-count // 8)
    pairs = count * (count + 1) // 2
    return pl.pallas_call(
        functools.partial(gram_kernel, count=count, opening=opening),
        grid_spec=pltpu.PrefetchScalarGridSpec(
            num_scalar_prefetch=1,
            grid=(steps,),
            in_specs=[pl.BlockSpec(before.shape, lambda i, h: (0, 0))]
            + [pl.BlockSpec(block, place)] * count,
            out_specs=pl.BlockSpec((rows, 128), lambda i, h: (0, 0)),
            scratch_shapes=[pltpu.VMEM((pairs, 8, 128), f32)],
        ),
        out_shape=jax.ShapeDtypeStruct((rows, 128), f32),
        compiler_params=pltpu.CompilerParams(vmem_limit_bytes=GRAM_LIMIT),
    )(info, before, *group)


def tree_weights(table, member, count):
    row = lax.broadcasted_iota(jnp.int32, table.shape, 0)
    lane = lax.broadcasted_iota(jnp.int32, table.shape, 1)

    def entry(a, b):
        picked = jnp.where((row == a) & (lane == b), table, 0.0)
        return jnp.sum(jnp.sum(picked, axis=1, keepdims=True), axis=0, keepdims=True)

    weights = [1.0 / entry(member ^ j, count) for j in range(count)]
    gram = {}
    for j in range(count):
        for k in range(j, count):
            gram[j, k] = entry(member ^ j, member ^ k) * weights[j] * weights[k]
    left = count
    while left > 1:
        bit = left // 2
        low, high = [], []
        for j in range(bit):
            norm_low = jnp.maximum(gram[j, j], 0.0)
            norm_high = jnp.maximum(gram[j + bit, j + bit], 0.0)
            limit = jnp.sqrt(norm_low) * jnp.sqrt(norm_high)
            product = jnp.clip(gram[j, j + bit], -limit, limit)
            low.append(1.0 - product / (2.0 * (norm_low + eps_adasum)))
            high.append(1.0 - product / (2.0 * (norm_high + eps_adasum)))
        for j in range(count):
            weights[j] = weights[j] * (high if j & bit else low)[j % bit]
        gram = {
            (j, k): low[j] * low[k] * gram[j, k]
            + high[j] * high[k] * gram[j + bit, k + bit]
            + (low[j] * high[k] * gram[j, k + bit] + low[k] * high[j] * gram[k, j + bit])
            for j in range(bit)
            for k in range(j, bit)
        }
        left = bit
    return weights


def update_kernel(info_ref, mine_ref, theirs_ref, *refs, count):
    firsts, seconds = refs[:count], refs[count : 2 * count]
    w1_ref, w2_ref, m1_ref, m2_ref, v1_ref, v2_ref = refs[2 * count : 2 * count + 6]
    outs, weight_ref = refs[2 * count + 6 : -1], refs[-1]

    @pl.when(pl.program_id(0) == 0)
    def _():
        weights = tree_weights(mine_ref[...] + theirs_ref[...], info_ref[0], count)
        for j in range(count):
            weight_ref[j : j + 1, :] = jnp.broadcast_to(weights[j], (1, 128))

    def combine(group):
        return sum(group[j][...] * weight_ref[j : j + 1, 0:1] for j in range(count))

    grad = combine(firsts)
    new = adam_update(grad, w1_ref[0].astype(f32), m1_ref[0], v1_ref[0])
    for n in range(3):
        outs[2 * n][0] = new[n]
    grad = combine(seconds).T
    new = adam_update(grad, w2_ref[0].astype(f32), m2_ref[0], v2_ref[0])
    for n in range(3):
        outs[2 * n + 1][0] = new[n]


def update_call(info, mine, theirs, firsts, seconds, w1, w2, m1, m2, v1, v2):
    count = len(firsts)
    steps = 6
    rows_first, hidden_width = firsts[0].shape
    width, rows_second = seconds[0].shape
    first_block = (rows_first, hidden_width // steps)
    second_block = (width // steps, rows_second)
    first_own = pl.BlockSpec((1,) + first_block, lambda i, h: (0, 0, i))
    second_own = pl.BlockSpec((1, rows_second, width // steps), lambda i, h: (0, 0, i))
    return pl.pallas_call(
        functools.partial(update_kernel, count=count),
        grid_spec=pltpu.PrefetchScalarGridSpec(
            num_scalar_prefetch=1,
            grid=(steps,),
            in_specs=[pl.BlockSpec(mine.shape, lambda i, h: (0, 0))] * 2
            + [pl.BlockSpec(first_block, lambda i, h: (0, i))] * count
            + [pl.BlockSpec(second_block, lambda i, h: (i, 0))] * count
            + [
                pl.BlockSpec((1,) + first_block, lambda i, h: (0, h[1], i)),
                pl.BlockSpec((1, rows_second, width // steps), lambda i, h: (0, h[1], i)),
            ]
            + [first_own, second_own] * 2,
            out_specs=[first_own, second_own] * 3,
            scratch_shapes=[pltpu.VMEM((8 * -(-count // 8), 128), f32)],
        ),
        out_shape=[
            jax.ShapeDtypeStruct((1, rows_first, hidden_width), f32),
            jax.ShapeDtypeStruct((1, rows_second, width), f32),
        ]
        * 3,
        compiler_params=pltpu.CompilerParams(vmem_limit_bytes=UPDATE_LIMIT),
    )(info, mine, theirs, *firsts, *seconds, w1, w2, m1, m2, v1, v2)


def after(value, *others):
    return lax.optimization_barrier((value, *others))[0]


def body(
    tokens,
    assigned,
    gate_prob,
    cotangent,
    weight_in,
    weight_out,
    moment_in,
    moment_out,
    second_in,
    second_out,
):
    experts = lax.axis_size("expert")
    replicas = lax.axis_size("dp")
    top = replicas // 2
    self_index = lax.axis_index("dp")
    expert = lax.axis_index("expert")
    half = self_index // top
    member = self_index % top
    tok_rows, width = tokens.shape
    hidden_width = weight_in.shape[2]
    capacity = 2 * tok_rows // experts
    rows_first = width // replicas
    rows_second = hidden_width // replicas
    w_first = weight_in[0]
    w_second = weight_out[0]
    info = jnp.stack([member, self_index, half]).astype(jnp.int32)

    ids = assigned.reshape(-1, 128)
    far_ids = swap(ids, "dp", top)
    scaled = (after(gate_prob, ids) * cotangent.astype(f32)).astype(bf16)
    far_scaled = swap(scaled, "dp", top)
    table = slot_table(assigned, expert, experts, capacity)
    upstream, own_sent = dispatch(table, scaled, experts)
    inputs = dispatch(table, after(tokens, *own_sent), experts)[0]
    far_tokens = swap(after(tokens, upstream), "dp", top)

    far_table = slot_table(far_ids.reshape(-1, 1), expert, experts, capacity)
    own_in, own_out, partial_out = expert_call(
        "first", info, after(inputs, upstream), upstream, w_first, w_second
    )
    far_scaled = after(far_scaled, partial_out)
    far_upstream = dispatch(far_table, far_scaled, experts)[0]
    far_tokens = after(far_tokens, partial_out)
    far_inputs, far_sent = dispatch(far_table, far_tokens, experts)
    own_in, expert_out = expert_call(
        "second",
        info,
        inputs,
        upstream,
        w_first,
        w_second,
        after(partial_out, *far_sent),
        own_in,
    )

    expert_out = after(expert_out, far_upstream)
    returned = exchange_blocks(
        [expert_out[j * capacity : (j + 1) * capacity] for j in range(experts)]
    )
    far_in, far_out, mine = expert_call(
        "far", info, far_inputs, far_upstream, w_first, w_second, own_in, own_out
    )
    mine = after(mine, returned)

    theirs = swap(mine, "dp", top)
    cross = mine[0] + theirs[0]
    norm_own = mine[1] + theirs[2]
    norm_far = mine[2] + theirs[1]
    coef_own = 1.0 - cross / (2.0 * (norm_own + eps_adasum))
    coef_far = 1.0 - cross / (2.0 * (norm_far + eps_adasum))
    weighted = coef_own * coef_own * norm_own + coef_far * coef_far * norm_far
    norm = jnp.maximum(weighted + 2.0 * coef_own * coef_far * cross, 1e-5 * weighted)
    scale = 16384.0 * lax.rsqrt(jnp.maximum(norm, 1e-12))
    weight_own, weight_far = coef_own * scale, coef_far * scale

    def quarter(own, far, other, axis):
        size = own.shape[axis] // top
        own, far = (
            lax.dynamic_slice_in_dim(x, (member ^ other) * size, size, axis) for x in (own, far)
        )
        return weight_own[0] * own + weight_far[0] * far

    def exchange(own, far, axis):
        received = [quarter(own, far, 0, axis)]
        for other in range(1, top):
            outgoing = quarter(own, far, other, axis).astype(f16)
            received.append(swap(outgoing, "dp", other).astype(f32))
        return received

    firsts = exchange(own_in, far_in, 0)
    seconds = exchange(own_out, far_out, 1)

    products = gram_call(info, scale.reshape(1, 128), firsts, True)
    products = gram_call(info, products, seconds, False)
    bit = 1
    while bit < top:
        products = products + swap(products, "dp", bit)
        bit *= 2
    new = update_call(
        info,
        products,
        swap(products, "dp", top),
        firsts,
        seconds,
        weight_in,
        weight_out,
        moment_in,
        moment_out,
        second_in,
        second_out,
    )

    picked = contract_rows(table, jnp.concatenate(returned, axis=0))
    combined = (gate_prob * picked).astype(bf16)
    return (combined, *new)


def solution(mesh):
    row_spec = P(("dp", "expert"), None)
    owner_spec = P("expert", "dp", None)
    return jax.shard_map(
        body,
        mesh=mesh,
        in_specs=(row_spec,) * 4 + (P("expert", None, None),) * 2 + (owner_spec,) * 4,
        out_specs=(row_spec,) + (owner_spec,) * 6,
        check_vma=False,
    )
```

```python
import functools

import jax
import jax.numpy as jnp
from jax import lax
from jax.experimental import pallas as pl
from jax.experimental.pallas import tpu as pltpu
from jax.sharding import PartitionSpec as P

eps_adasum = 1e-06
f32 = jnp.float32
bf16 = jnp.bfloat16
f16 = jnp.float16
VMEM_LIMIT = 48 << 20
GRAM_LIMIT = 8 << 20
UPDATE_LIMIT = 20 << 20
COST = 1 << 10
COST = 1 << 10
TOKEN_PIECES = 1
SCALED_PIECES = 1
CHAIN = False


def swap(x, axis, offset):
    return lax.ppermute(x, axis, [(i, i ^ offset) for i in range(lax.axis_size(axis))])


def gelu_and_slope(values):
    root = 0.7978845608028654
    square = values * values
    tanh = jnp.tanh(values * (root + (root * 0.044715) * square))
    cdf = 0.5 + 0.5 * tanh
    slope = cdf + (0.5 * values) * (1.0 - tanh * tanh) * (root + (3.0 * root * 0.044715) * square)
    return values * cdf, slope


def adam_update(grad, weight, moment, second):
    new_moment = 0.9 * moment + 0.1 * grad
    new_second = 0.999 * second + 0.001 * grad * grad
    corr_one = 1.0 - 0.9**10.0
    corr_two = 1.0 - 0.999**10.0
    update = new_moment / corr_one / (jnp.sqrt(new_second / corr_two) + 1e-08)
    return (weight - 0.001 * update, new_moment, new_second)


def contract_rows(left, right):
    return lax.dot_general(
        left, right, (((0,), (0,)), ((), ())), preferred_element_type=f32
    )


def slot_table(assigned, expert, experts, capacity):
    expert_ids = assigned[:, 0]
    one_hot = (expert_ids[:, None] == jnp.arange(experts, dtype=jnp.int32)[None, :]).astype(
        jnp.int32
    )
    slot_index = jnp.sum((jnp.cumsum(one_hot, axis=0) - one_hot) * one_hot, axis=1)
    slot_code = (expert_ids ^ expert) * capacity + slot_index
    rows = experts * capacity
    return (jnp.arange(rows, dtype=jnp.int32)[:, None] == slot_code[None, :]).astype(bf16)


def exchange_blocks(blocks):
    return [blocks[0]] + [swap(blocks[j], "expert", j) for j in range(1, len(blocks))]


def place_rows(table, rows, experts):
    capacity = table.shape[0] // experts
    sent = jnp.dot(table, rows, preferred_element_type=f32).astype(bf16)
    return [sent[j * capacity : (j + 1) * capacity] for j in range(experts)]


def dispatch(table, rows, experts):
    placed = place_rows(table, rows, experts)
    return jnp.concatenate(exchange_blocks(placed), axis=0), placed


def fold(values):
    rows = values.reshape(values.shape[0] // 8, 8, values.shape[1]).sum(0)
    spare = -rows.shape[1] % 128
    if spare:
        rows = jnp.concatenate([rows, jnp.zeros((8, spare), f32)], axis=1)
    return sum(rows[:, k * 128 : (k + 1) * 128] for k in range(rows.shape[1] // 128))


def expert_kernel(info_ref, x_ref, u_ref, w1_ref, w2_ref, *rest, steps, kind):
    if kind == "first":
        gi_ref, go_ref, sum_ref, xt_ref, ut_ref = rest
    elif kind == "middle":
        before_ref, _, _, gi_ref, go_ref, sum_ref, xt_ref = rest
    elif kind == "last":
        before_ref, _, gi_ref, out_ref, xt_ref, sum_ref = rest
    else:
        own_gi_ref, own_go_ref, gi_ref, go_ref, stat_ref, xt_ref, ut_ref, acc_ref = rest
    step = pl.program_id(0)
    half_width = xt_ref.shape[0]

    @pl.when(step == 0)
    def _():
        start = pl.multiple_of(info_ref[2] * half_width, half_width)
        xt_ref[...] = x_ref[:, pl.ds(start, half_width)].T
        if kind in ("first", "far"):
            ut_ref[...] = u_ref[...].T

    pre = jnp.dot(x_ref[...], w1_ref[...], preferred_element_type=f32)
    back = lax.dot_general(
        u_ref[...], w2_ref[...], (((1,), (1,)), ((), ())), preferred_element_type=f32
    )
    act, slope = gelu_and_slope(pre)
    hidden = act.astype(bf16)
    hidden_grad = (slope * back).astype(bf16)
    gi_ref[...] = jnp.dot(xt_ref[...], hidden_grad, preferred_element_type=f32)

    if kind == "first":
        go_ref[...] = jnp.dot(ut_ref[...], hidden, preferred_element_type=f32)
    elif kind == "middle":
        go_ref[...] = jnp.dot(u_ref[...].T, hidden, preferred_element_type=f32)

    elif kind == "far":

        @pl.when(step < steps // 2)
        def _():
            go_ref[...] = jnp.dot(ut_ref[...], hidden, preferred_element_type=f32)

    if kind == "far":

        def add(mine, far):
            acc_ref[0] += fold(mine * far)
            acc_ref[1] += fold(mine * mine)
            acc_ref[2] += fold(far * far)

        @pl.when(step == 0)
        def _():
            acc_ref[...] = jnp.zeros_like(acc_ref)

        add(own_gi_ref[...], gi_ref[...])

        @pl.when(step < steps // 2)
        def _():
            add(own_go_ref[...], go_ref[...])

        @pl.when(step == steps - 1)
        def _():
            row = lax.broadcasted_iota(jnp.int32, (8, 128), 0)
            stats = jnp.zeros((8, 128), f32)
            for k in range(3):
                stats = jnp.where(row == k, jnp.sum(acc_ref[k]), stats)
            stat_ref[...] = stats

    else:
        product = jnp.dot(hidden, w2_ref[...], preferred_element_type=f32)

        @pl.when(step == 0)
        def _():
            sum_ref[...] = product if kind == "first" else before_ref[...] + product

        @pl.when(step > 0)
        def _():
            sum_ref[...] += product

        if kind == "last":

            @pl.when(step == steps // 2 - 1)
            def _():
                out_ref[...] = sum_ref[...].astype(bf16)


def expert_call(kind, info, x, u, w1, w2, *previous):
    rows, width = x.shape
    hidden_width = w1.shape[1]
    steps = 6
    block = hidden_width // steps
    half_steps = steps // 2
    shift = {"first": 0, "middle": half_steps - 1, "last": half_steps, "far": 0}[kind]
    count = {"first": half_steps - 1, "middle": 1, "last": half_steps, "far": steps}[kind]

    def column(i, h):
        return (0, (i + shift + h[2] * (steps // 2)) % steps)

    def row(i, h):
        return ((i + shift + h[2] * (steps // 2)) % steps, 0)

    def held(i, h):
        return (0, jnp.minimum(i + shift, steps // 2 - 1))

    def whole(i, h):
        return (0, 0)

    one = pl.Buffered(1)
    whole_spec = pl.BlockSpec((rows, width), whole, pipeline_mode=one)
    in_specs = [
        whole_spec,
        whole_spec,
        pl.BlockSpec((width, block), column),
        pl.BlockSpec((block, width), row),
    ]
    gi_spec = pl.BlockSpec((width // 2, block), column)
    go_spec = pl.BlockSpec((width, block), held)
    gi_shape = jax.ShapeDtypeStruct((width // 2, hidden_width), f32)
    go_shape = jax.ShapeDtypeStruct((width, hidden_width // 2), f32)
    sum_shape = jax.ShapeDtypeStruct((rows, width), f32)
    xt = pltpu.VMEM((width // 2, rows), bf16)
    ut = pltpu.VMEM((width, rows), bf16)
    aliases = {}
    if kind == "first":
        out_specs = [gi_spec, go_spec, whole_spec]
        out_shape = [gi_shape, go_shape, sum_shape]
        scratch = [xt, ut]
    elif kind == "middle":
        in_specs += [whole_spec] + [pl.BlockSpec(memory_space=pl.ANY)] * 2
        out_specs = [gi_spec, go_spec, whole_spec]
        out_shape = [gi_shape, go_shape, sum_shape]
        scratch = [xt]
        aliases = {6: 0, 7: 1}
    elif kind == "last":
        in_specs += [whole_spec, pl.BlockSpec(memory_space=pl.ANY)]
        out_specs = [gi_spec, whole_spec]
        out_shape = [gi_shape, jax.ShapeDtypeStruct((rows, width), bf16)]
        scratch = [xt, pltpu.VMEM((rows, width), f32)]
        aliases = {6: 0}
    else:
        in_specs += [gi_spec, go_spec]
        out_specs = [gi_spec, go_spec, pl.BlockSpec((8, 128), whole)]
        out_shape = [gi_shape, go_shape, jax.ShapeDtypeStruct((8, 128), f32)]
        scratch = [xt, ut, pltpu.VMEM((3, 8, 128), f32)]
    return pl.pallas_call(
        functools.partial(expert_kernel, steps=steps, kind=kind),
        grid_spec=pltpu.PrefetchScalarGridSpec(
            num_scalar_prefetch=1,
            grid=(count,),
            in_specs=in_specs,
            out_specs=out_specs,
            scratch_shapes=scratch,
        ),
        out_shape=out_shape,
        input_output_aliases=aliases,
        compiler_params=pltpu.CompilerParams(vmem_limit_bytes=VMEM_LIMIT),
        cost_estimate=pl.CostEstimate(
            flops=COST, bytes_accessed=COST, transcendentals=0
        ),
    )(info, x, u, w1, w2, *previous)


def gram_kernel(info_ref, before_ref, *refs, count, opening):
    group, out_ref, acc_ref = refs[:count], refs[-2], refs[-1]
    step = pl.program_id(0)
    pairs = [(j, k) for j in range(count) for k in range(j, count)]

    @pl.when(step == 0)
    def _():
        acc_ref[...] = jnp.zeros_like(acc_ref)

    values = [ref[...] for ref in group]
    for n, (j, k) in enumerate(pairs):
        acc_ref[n] += fold(values[j] * values[k])

    @pl.when(step == pl.num_programs(0) - 1)
    def _():
        member = info_ref[0]
        row = lax.broadcasted_iota(jnp.int32, out_ref.shape, 0)
        lane = lax.broadcasted_iota(jnp.int32, out_ref.shape, 1)
        table = jnp.zeros(out_ref.shape, f32)
        if opening:
            table = jnp.where((row == member) & (lane == count), 0.5 * before_ref[...], 0.0)
        for n, (j, k) in enumerate(pairs):
            total = jnp.sum(acc_ref[n])
            a, b = member ^ j, member ^ k
            here = ((row == a) & (lane == b)) | ((row == b) & (lane == a))
            table = jnp.where(here, total, table)
        out_ref[...] = table if opening else table + before_ref[...]


def gram_call(info, before, group, opening):
    count = len(group)
    steps = 3
    if opening:
        block, place = (group[0].shape[0], group[0].shape[1] // steps), lambda i, h: (0, i)
    else:
        block, place = (group[0].shape[0] // steps, group[0].shape[1]), lambda i, h: (i, 0)
    rows = 8 * -(-count // 8)
    pairs = count * (count + 1) // 2
    return pl.pallas_call(
        functools.partial(gram_kernel, count=count, opening=opening),
        grid_spec=pltpu.PrefetchScalarGridSpec(
            num_scalar_prefetch=1,
            grid=(steps,),
            in_specs=[pl.BlockSpec(before.shape, lambda i, h: (0, 0))]
            + [pl.BlockSpec(block, place)] * count,
            out_specs=pl.BlockSpec((rows, 128), lambda i, h: (0, 0)),
            scratch_shapes=[pltpu.VMEM((pairs, 8, 128), f32)],
        ),
        out_shape=jax.ShapeDtypeStruct((rows, 128), f32),
        compiler_params=pltpu.CompilerParams(vmem_limit_bytes=GRAM_LIMIT),
    )(info, before, *group)


def tree_weights(table, member, count):
    row = lax.broadcasted_iota(jnp.int32, table.shape, 0)
    lane = lax.broadcasted_iota(jnp.int32, table.shape, 1)

    def entry(a, b):
        picked = jnp.where((row == a) & (lane == b), table, 0.0)
        return jnp.sum(jnp.sum(picked, axis=1, keepdims=True), axis=0, keepdims=True)

    weights = [1.0 / entry(member ^ j, count) for j in range(count)]
    gram = {}
    for j in range(count):
        for k in range(j, count):
            gram[j, k] = entry(member ^ j, member ^ k) * weights[j] * weights[k]
    left = count
    while left > 1:
        bit = left // 2
        low, high = [], []
        for j in range(bit):
            norm_low = jnp.maximum(gram[j, j], 0.0)
            norm_high = jnp.maximum(gram[j + bit, j + bit], 0.0)
            limit = jnp.sqrt(norm_low) * jnp.sqrt(norm_high)
            product = jnp.clip(gram[j, j + bit], -limit, limit)
            low.append(1.0 - product / (2.0 * (norm_low + eps_adasum)))
            high.append(1.0 - product / (2.0 * (norm_high + eps_adasum)))
        for j in range(count):
            weights[j] = weights[j] * (high if j & bit else low)[j % bit]
        gram = {
            (j, k): low[j] * low[k] * gram[j, k]
            + high[j] * high[k] * gram[j + bit, k + bit]
            + (low[j] * high[k] * gram[j, k + bit] + low[k] * high[j] * gram[k, j + bit])
            for j in range(bit)
            for k in range(j, bit)
        }
        left = bit
    return weights


def update_kernel(info_ref, mine_ref, theirs_ref, *refs, count):
    firsts, seconds = refs[:count], refs[count : 2 * count]
    w1_ref, w2_ref, m1_ref, m2_ref, v1_ref, v2_ref = refs[2 * count : 2 * count + 6]
    outs, weight_ref = refs[2 * count + 6 : -1], refs[-1]

    @pl.when(pl.program_id(0) == 0)
    def _():
        weights = tree_weights(mine_ref[...] + theirs_ref[...], info_ref[0], count)
        for j in range(count):
            weight_ref[j : j + 1, :] = jnp.broadcast_to(weights[j], (1, 128))

    def combine(group):
        return sum(group[j][...] * weight_ref[j : j + 1, 0:1] for j in range(count))

    grad = combine(firsts)
    new = adam_update(grad, w1_ref[0].astype(f32), m1_ref[0], v1_ref[0])
    for n in range(3):
        outs[2 * n][0] = new[n]
    grad = combine(seconds).T
    new = adam_update(grad, w2_ref[0].astype(f32), m2_ref[0], v2_ref[0])
    for n in range(3):
        outs[2 * n + 1][0] = new[n]


def update_call(info, mine, theirs, firsts, seconds, w1, w2, m1, m2, v1, v2):
    count = len(firsts)
    steps = 6
    rows_first, hidden_width = firsts[0].shape
    width, rows_second = seconds[0].shape
    first_block = (rows_first, hidden_width // steps)
    second_block = (width // steps, rows_second)
    first_own = pl.BlockSpec((1,) + first_block, lambda i, h: (0, 0, i))
    second_own = pl.BlockSpec((1, rows_second, width // steps), lambda i, h: (0, 0, i))
    return pl.pallas_call(
        functools.partial(update_kernel, count=count),
        grid_spec=pltpu.PrefetchScalarGridSpec(
            num_scalar_prefetch=1,
            grid=(steps,),
            in_specs=[pl.BlockSpec(mine.shape, lambda i, h: (0, 0))] * 2
            + [pl.BlockSpec(first_block, lambda i, h: (0, i))] * count
            + [pl.BlockSpec(second_block, lambda i, h: (i, 0))] * count
            + [
                pl.BlockSpec((1,) + first_block, lambda i, h: (0, h[1], i)),
                pl.BlockSpec((1, rows_second, width // steps), lambda i, h: (0, h[1], i)),
            ]
            + [first_own, second_own] * 2,
            out_specs=[first_own, second_own] * 3,
            scratch_shapes=[pltpu.VMEM((8 * -(-count // 8), 128), f32)],
        ),
        out_shape=[
            jax.ShapeDtypeStruct((1, rows_first, hidden_width), f32),
            jax.ShapeDtypeStruct((1, rows_second, width), f32),
        ]
        * 3,
        compiler_params=pltpu.CompilerParams(vmem_limit_bytes=UPDATE_LIMIT),
    )(info, mine, theirs, *firsts, *seconds, w1, w2, m1, m2, v1, v2)


def after(value, *others):
    return lax.optimization_barrier((value, *others))[0]


def body(
    tokens,
    assigned,
    gate_prob,
    cotangent,
    weight_in,
    weight_out,
    moment_in,
    moment_out,
    second_in,
    second_out,
):
    experts = lax.axis_size("expert")
    replicas = lax.axis_size("dp")
    top = replicas // 2
    self_index = lax.axis_index("dp")
    expert = lax.axis_index("expert")
    half = self_index // top
    member = self_index % top
    tok_rows, width = tokens.shape
    hidden_width = weight_in.shape[2]
    capacity = 2 * tok_rows // experts
    rows_first = width // replicas
    rows_second = hidden_width // replicas
    w_first = weight_in[0]
    w_second = weight_out[0]
    info = jnp.stack([member, self_index, half]).astype(jnp.int32)

    ids = assigned.reshape(-1, 128)
    far_ids = swap(ids, "dp", top)
    scaled = (after(gate_prob, ids) * cotangent.astype(f32)).astype(bf16)
    far_scaled = swap(scaled, "dp", top)
    table = slot_table(assigned, expert, experts, capacity)
    upstream, own_sent = dispatch(table, scaled, experts)
    inputs = dispatch(table, after(tokens, *own_sent), experts)[0]
    far_tokens = swap(after(tokens, upstream), "dp", top)

    far_table = slot_table(far_ids.reshape(-1, 1), expert, experts, capacity)
    own_in, own_out, partial_out = expert_call(
        "first", info, after(inputs, upstream), upstream, w_first, w_second
    )
    far_scaled = after(far_scaled, partial_out)
    far_upstream, far_sent = dispatch(far_table, far_scaled, experts)
    own_in, own_out, partial_out = expert_call(
        "middle",
        info,
        inputs,
        upstream,
        w_first,
        w_second,
        after(partial_out, *far_sent),
        own_in,
        own_out,
    )
    far_tokens = after(far_tokens, partial_out)
    far_inputs, far_sent = dispatch(far_table, far_tokens, experts)
    own_in, expert_out = expert_call(
        "last",
        info,
        inputs,
        upstream,
        w_first,
        w_second,
        after(partial_out, *far_sent),
        own_in,
    )

    expert_out = after(expert_out, far_upstream, far_inputs)
    returned = exchange_blocks(
        [expert_out[j * capacity : (j + 1) * capacity] for j in range(experts)]
    )
    far_in, far_out, mine = expert_call(
        "far", info, far_inputs, far_upstream, w_first, w_second, own_in, own_out
    )
    mine = after(mine, returned)

    theirs = swap(mine, "dp", top)
    cross = mine[0] + theirs[0]
    norm_own = mine[1] + theirs[2]
    norm_far = mine[2] + theirs[1]
    coef_own = 1.0 - cross / (2.0 * (norm_own + eps_adasum))
    coef_far = 1.0 - cross / (2.0 * (norm_far + eps_adasum))
    weighted = coef_own * coef_own * norm_own + coef_far * coef_far * norm_far
    norm = jnp.maximum(weighted + 2.0 * coef_own * coef_far * cross, 1e-5 * weighted)
    scale = 16384.0 * lax.rsqrt(jnp.maximum(norm, 1e-12))
    weight_own, weight_far = coef_own * scale, coef_far * scale

    def quarter(own, far, other, axis, left, right):
        size = own.shape[axis] // top
        own, far = (
            lax.dynamic_slice_in_dim(x, (member ^ other) * size, size, axis) for x in (own, far)
        )
        return left * own + right * far

    def exchange(own, far, axis):
        pair = (weight_own[0], weight_far[0])
        others = range(1, top)
        outgoing = [quarter(own, far, other, axis, *pair).astype(f16) for other in others]
        if axis == 0:
            pair = [after(weight, *outgoing) for weight in pair]
        received = [swap(x, "dp", other).astype(f32) for x, other in zip(outgoing, others)]
        return [quarter(own, far, 0, axis, *pair)] + received

    firsts = exchange(own_in, far_in, 0)
    seconds = exchange(own_out, far_out, 1)

    products = gram_call(info, scale.reshape(1, 128), firsts, True)
    products = gram_call(info, products, seconds, False)
    bit = 1
    while bit < top:
        products = products + swap(products, "dp", bit)
        bit *= 2
    new = update_call(
        info,
        products,
        swap(products, "dp", top),
        firsts,
        seconds,
        weight_in,
        weight_out,
        moment_in,
        moment_out,
        second_in,
        second_out,
    )

    picked = contract_rows(table, jnp.concatenate(returned, axis=0))
    combined = (gate_prob * picked).astype(bf16)
    return (combined, *new)


def solution(mesh):
    row_spec = P(("dp", "expert"), None)
    owner_spec = P("expert", "dp", None)
    return jax.shard_map(
        body,
        mesh=mesh,
        in_specs=(row_spec,) * 4 + (P("expert", None, None),) * 2 + (owner_spec,) * 4,
        out_specs=(row_spec,) + (owner_spec,) * 6,
        check_vma=False,
    )
```

```python
import functools

import jax
import jax.numpy as jnp
from jax import lax
from jax.experimental import pallas as pl
from jax.experimental.pallas import tpu as pltpu
from jax.sharding import PartitionSpec as P

eps_adasum = 1e-06
f32 = jnp.float32
bf16 = jnp.bfloat16
f16 = jnp.float16
VMEM_LIMIT = 48 << 20
GRAM_LIMIT = 8 << 20
UPDATE_LIMIT = 20 << 20
COST = 1 << 10
COST = 1 << 10
TOKEN_PIECES = 1
SCALED_PIECES = 1
CHAIN = False


def swap(x, axis, offset):
    return lax.ppermute(x, axis, [(i, i ^ offset) for i in range(lax.axis_size(axis))])


def gelu_and_slope(values):
    root = 0.7978845608028654
    square = values * values
    tanh = jnp.tanh(values * (root + (root * 0.044715) * square))
    cdf = 0.5 + 0.5 * tanh
    slope = cdf + (0.5 * values) * (1.0 - tanh * tanh) * (root + (3.0 * root * 0.044715) * square)
    return values * cdf, slope


def adam_update(grad, weight, moment, second):
    new_moment = 0.9 * moment + 0.1 * grad
    new_second = 0.999 * second + 0.001 * grad * grad
    corr_one = 1.0 - 0.9**10.0
    corr_two = 1.0 - 0.999**10.0
    update = new_moment / corr_one / (jnp.sqrt(new_second / corr_two) + 1e-08)
    return (weight - 0.001 * update, new_moment, new_second)


def contract_rows(left, right):
    return lax.dot_general(
        left, right, (((0,), (0,)), ((), ())), preferred_element_type=f32
    )


def slot_table(assigned, expert, experts, capacity):
    expert_ids = assigned[:, 0]
    one_hot = (expert_ids[:, None] == jnp.arange(experts, dtype=jnp.int32)[None, :]).astype(
        jnp.int32
    )
    slot_index = jnp.sum((jnp.cumsum(one_hot, axis=0) - one_hot) * one_hot, axis=1)
    slot_code = (expert_ids ^ expert) * capacity + slot_index
    rows = experts * capacity
    return (jnp.arange(rows, dtype=jnp.int32)[:, None] == slot_code[None, :]).astype(bf16)


def exchange_blocks(blocks):
    return [blocks[0]] + [swap(blocks[j], "expert", j) for j in range(1, len(blocks))]


def place_rows(table, rows, experts):
    capacity = table.shape[0] // experts
    sent = jnp.dot(table, rows, preferred_element_type=f32).astype(bf16)
    return [sent[j * capacity : (j + 1) * capacity] for j in range(experts)]


def dispatch(table, rows, experts):
    placed = place_rows(table, rows, experts)
    return jnp.concatenate(exchange_blocks(placed), axis=0), placed


def fold(values):
    rows = values.reshape(values.shape[0] // 8, 8, values.shape[1]).sum(0)
    spare = -rows.shape[1] % 128
    if spare:
        rows = jnp.concatenate([rows, jnp.zeros((8, spare), f32)], axis=1)
    return sum(rows[:, k * 128 : (k + 1) * 128] for k in range(rows.shape[1] // 128))


def expert_kernel(info_ref, x_ref, u_ref, w1_ref, w2_ref, *rest, steps, kind):
    if kind == "first":
        gi_ref, go_ref, sum_ref, xt_ref, ut_ref = rest
    elif kind == "middle":
        before_ref, _, _, gi_ref, go_ref, sum_ref, xt_ref = rest
    elif kind == "last":
        before_ref, _, gi_ref, out_ref, xt_ref, sum_ref = rest
    else:
        own_gi_ref, own_go_ref, gi_ref, go_ref, stat_ref, xt_ref, ut_ref, acc_ref = rest
    step = pl.program_id(0)
    half_width = xt_ref.shape[0]

    @pl.when(step == 0)
    def _():
        start = pl.multiple_of(info_ref[2] * half_width, half_width)
        xt_ref[...] = x_ref[:, pl.ds(start, half_width)].T
        if kind in ("first", "far"):
            ut_ref[...] = u_ref[...].T

    pre = jnp.dot(x_ref[...], w1_ref[...], preferred_element_type=f32)
    back = lax.dot_general(
        u_ref[...], w2_ref[...], (((1,), (1,)), ((), ())), preferred_element_type=f32
    )
    act, slope = gelu_and_slope(pre)
    hidden = act.astype(bf16)
    hidden_grad = (slope * back).astype(bf16)
    gi_ref[...] = jnp.dot(xt_ref[...], hidden_grad, preferred_element_type=f32)

    if kind == "first":
        go_ref[...] = jnp.dot(ut_ref[...], hidden, preferred_element_type=f32)
    elif kind == "middle":
        go_ref[...] = jnp.dot(u_ref[...].T, hidden, preferred_element_type=f32)

    elif kind == "far":

        @pl.when(step < steps // 2)
        def _():
            go_ref[...] = jnp.dot(ut_ref[...], hidden, preferred_element_type=f32)

    if kind == "far":

        def add(mine, far):
            acc_ref[0] += fold(mine * far)
            acc_ref[1] += fold(mine * mine)
            acc_ref[2] += fold(far * far)

        @pl.when(step == 0)
        def _():
            acc_ref[...] = jnp.zeros_like(acc_ref)

        add(own_gi_ref[...], gi_ref[...])

        @pl.when(step < steps // 2)
        def _():
            add(own_go_ref[...], go_ref[...])

        @pl.when(step == steps - 1)
        def _():
            row = lax.broadcasted_iota(jnp.int32, (8, 128), 0)
            stats = jnp.zeros((8, 128), f32)
            for k in range(3):
                stats = jnp.where(row == k, jnp.sum(acc_ref[k]), stats)
            stat_ref[...] = stats

    else:
        product = jnp.dot(hidden, w2_ref[...], preferred_element_type=f32)

        @pl.when(step == 0)
        def _():
            sum_ref[...] = product if kind == "first" else before_ref[...] + product

        @pl.when(step > 0)
        def _():
            sum_ref[...] += product

        if kind == "last":

            @pl.when(step == steps // 2 - 1)
            def _():
                out_ref[...] = sum_ref[...].astype(bf16)


def expert_call(kind, info, x, u, w1, w2, *previous):
    rows, width = x.shape
    hidden_width = w1.shape[1]
    steps = 6
    block = hidden_width // steps
    half_steps = steps // 2
    shift = {"first": 0, "middle": half_steps - 1, "last": half_steps, "far": 0}[kind]
    count = {"first": half_steps - 1, "middle": 1, "last": half_steps, "far": steps}[kind]

    def column(i, h):
        return (0, (i + shift + h[2] * (steps // 2)) % steps)

    def row(i, h):
        return ((i + shift + h[2] * (steps // 2)) % steps, 0)

    def held(i, h):
        return (0, jnp.minimum(i + shift, steps // 2 - 1))

    def whole(i, h):
        return (0, 0)

    one = pl.Buffered(1)
    whole_spec = pl.BlockSpec((rows, width), whole, pipeline_mode=one)
    in_specs = [
        pl.BlockSpec(memory_space=pltpu.VMEM),
        pl.BlockSpec(memory_space=pltpu.VMEM),
        pl.BlockSpec((width, block), column),
        pl.BlockSpec((block, width), row),
    ]
    gi_spec = pl.BlockSpec((width // 2, block), column)
    go_spec = pl.BlockSpec((width, block), held)
    gi_shape = jax.ShapeDtypeStruct((width // 2, hidden_width), f32)
    go_shape = jax.ShapeDtypeStruct((width, hidden_width // 2), f32)
    sum_shape = jax.ShapeDtypeStruct((rows, width), f32)
    xt = pltpu.VMEM((width // 2, rows), bf16)
    ut = pltpu.VMEM((width, rows), bf16)
    aliases = {}
    if kind == "first":
        out_specs = [gi_spec, go_spec, whole_spec]
        out_shape = [gi_shape, go_shape, sum_shape]
        scratch = [xt, ut]
    elif kind == "middle":
        in_specs += [whole_spec] + [pl.BlockSpec(memory_space=pl.ANY)] * 2
        out_specs = [gi_spec, go_spec, whole_spec]
        out_shape = [gi_shape, go_shape, sum_shape]
        scratch = [xt]
        aliases = {6: 0, 7: 1}
    elif kind == "last":
        in_specs += [whole_spec, pl.BlockSpec(memory_space=pl.ANY)]
        out_specs = [gi_spec, whole_spec]
        out_shape = [gi_shape, jax.ShapeDtypeStruct((rows, width), bf16)]
        scratch = [xt, pltpu.VMEM((rows, width), f32)]
        aliases = {6: 0}
    else:
        in_specs += [gi_spec, go_spec]
        out_specs = [gi_spec, go_spec, pl.BlockSpec((8, 128), whole)]
        out_shape = [gi_shape, go_shape, jax.ShapeDtypeStruct((8, 128), f32)]
        scratch = [xt, ut, pltpu.VMEM((3, 8, 128), f32)]
    return pl.pallas_call(
        functools.partial(expert_kernel, steps=steps, kind=kind),
        grid_spec=pltpu.PrefetchScalarGridSpec(
            num_scalar_prefetch=1,
            grid=(count,),
            in_specs=in_specs,
            out_specs=out_specs,
            scratch_shapes=scratch,
        ),
        out_shape=out_shape,
        input_output_aliases=aliases,
        compiler_params=pltpu.CompilerParams(vmem_limit_bytes=VMEM_LIMIT),
        cost_estimate=pl.CostEstimate(
            flops=COST, bytes_accessed=COST, transcendentals=0
        ),
    )(info, x, u, w1, w2, *previous)


def gram_kernel(info_ref, before_ref, *refs, count, opening):
    group, out_ref, acc_ref = refs[:count], refs[-2], refs[-1]
    step = pl.program_id(0)
    pairs = [(j, k) for j in range(count) for k in range(j, count)]

    @pl.when(step == 0)
    def _():
        acc_ref[...] = jnp.zeros_like(acc_ref)

    values = [ref[...] for ref in group]
    for n, (j, k) in enumerate(pairs):
        acc_ref[n] += fold(values[j] * values[k])

    @pl.when(step == pl.num_programs(0) - 1)
    def _():
        member = info_ref[0]
        row = lax.broadcasted_iota(jnp.int32, out_ref.shape, 0)
        lane = lax.broadcasted_iota(jnp.int32, out_ref.shape, 1)
        table = jnp.zeros(out_ref.shape, f32)
        if opening:
            table = jnp.where((row == member) & (lane == count), 0.5 * before_ref[...], 0.0)
        for n, (j, k) in enumerate(pairs):
            total = jnp.sum(acc_ref[n])
            a, b = member ^ j, member ^ k
            here = ((row == a) & (lane == b)) | ((row == b) & (lane == a))
            table = jnp.where(here, total, table)
        out_ref[...] = table if opening else table + before_ref[...]


def gram_call(info, before, group, opening):
    count = len(group)
    steps = 3
    if opening:
        block, place = (group[0].shape[0], group[0].shape[1] // steps), lambda i, h: (0, i)
    else:
        block, place = (group[0].shape[0] // steps, group[0].shape[1]), lambda i, h: (i, 0)
    rows = 8 * -(-count // 8)
    pairs = count * (count + 1) // 2
    return pl.pallas_call(
        functools.partial(gram_kernel, count=count, opening=opening),
        grid_spec=pltpu.PrefetchScalarGridSpec(
            num_scalar_prefetch=1,
            grid=(steps,),
            in_specs=[pl.BlockSpec(before.shape, lambda i, h: (0, 0))]
            + [pl.BlockSpec(block, place)] * count,
            out_specs=pl.BlockSpec((rows, 128), lambda i, h: (0, 0)),
            scratch_shapes=[pltpu.VMEM((pairs, 8, 128), f32)],
        ),
        out_shape=jax.ShapeDtypeStruct((rows, 128), f32),
        compiler_params=pltpu.CompilerParams(vmem_limit_bytes=GRAM_LIMIT),
    )(info, before, *group)


def tree_weights(table, member, count):
    row = lax.broadcasted_iota(jnp.int32, table.shape, 0)
    lane = lax.broadcasted_iota(jnp.int32, table.shape, 1)

    def entry(a, b):
        picked = jnp.where((row == a) & (lane == b), table, 0.0)
        return jnp.sum(jnp.sum(picked, axis=1, keepdims=True), axis=0, keepdims=True)

    weights = [1.0 / entry(member ^ j, count) for j in range(count)]
    gram = {}
    for j in range(count):
        for k in range(j, count):
            gram[j, k] = entry(member ^ j, member ^ k) * weights[j] * weights[k]
    left = count
    while left > 1:
        bit = left // 2
        low, high = [], []
        for j in range(bit):
            norm_low = jnp.maximum(gram[j, j], 0.0)
            norm_high = jnp.maximum(gram[j + bit, j + bit], 0.0)
            limit = jnp.sqrt(norm_low) * jnp.sqrt(norm_high)
            product = jnp.clip(gram[j, j + bit], -limit, limit)
            low.append(1.0 - product / (2.0 * (norm_low + eps_adasum)))
            high.append(1.0 - product / (2.0 * (norm_high + eps_adasum)))
        for j in range(count):
            weights[j] = weights[j] * (high if j & bit else low)[j % bit]
        gram = {
            (j, k): low[j] * low[k] * gram[j, k]
            + high[j] * high[k] * gram[j + bit, k + bit]
            + (low[j] * high[k] * gram[j, k + bit] + low[k] * high[j] * gram[k, j + bit])
            for j in range(bit)
            for k in range(j, bit)
        }
        left = bit
    return weights


def update_kernel(info_ref, mine_ref, theirs_ref, *refs, count):
    firsts, seconds = refs[:count], refs[count : 2 * count]
    w1_ref, w2_ref, m1_ref, m2_ref, v1_ref, v2_ref = refs[2 * count : 2 * count + 6]
    outs, weight_ref = refs[2 * count + 6 : -1], refs[-1]

    @pl.when(pl.program_id(0) == 0)
    def _():
        weights = tree_weights(mine_ref[...] + theirs_ref[...], info_ref[0], count)
        for j in range(count):
            weight_ref[j : j + 1, :] = jnp.broadcast_to(weights[j], (1, 128))

    def combine(group):
        return sum(group[j][...] * weight_ref[j : j + 1, 0:1] for j in range(count))

    grad = combine(firsts)
    new = adam_update(grad, w1_ref[0].astype(f32), m1_ref[0], v1_ref[0])
    for n in range(3):
        outs[2 * n][0] = new[n]
    grad = combine(seconds).T
    new = adam_update(grad, w2_ref[0].astype(f32), m2_ref[0], v2_ref[0])
    for n in range(3):
        outs[2 * n + 1][0] = new[n]


def update_call(info, mine, theirs, firsts, seconds, w1, w2, m1, m2, v1, v2):
    count = len(firsts)
    steps = 6
    rows_first, hidden_width = firsts[0].shape
    width, rows_second = seconds[0].shape
    first_block = (rows_first, hidden_width // steps)
    second_block = (width // steps, rows_second)
    first_own = pl.BlockSpec((1,) + first_block, lambda i, h: (0, 0, i))
    second_own = pl.BlockSpec((1, rows_second, width // steps), lambda i, h: (0, 0, i))
    return pl.pallas_call(
        functools.partial(update_kernel, count=count),
        grid_spec=pltpu.PrefetchScalarGridSpec(
            num_scalar_prefetch=1,
            grid=(steps,),
            in_specs=[pl.BlockSpec(mine.shape, lambda i, h: (0, 0))] * 2
            + [pl.BlockSpec(first_block, lambda i, h: (0, i))] * count
            + [pl.BlockSpec(second_block, lambda i, h: (i, 0))] * count
            + [
                pl.BlockSpec((1,) + first_block, lambda i, h: (0, h[1], i)),
                pl.BlockSpec((1, rows_second, width // steps), lambda i, h: (0, h[1], i)),
            ]
            + [first_own, second_own] * 2,
            out_specs=[first_own, second_own] * 3,
            scratch_shapes=[pltpu.VMEM((8 * -(-count // 8), 128), f32)],
        ),
        out_shape=[
            jax.ShapeDtypeStruct((1, rows_first, hidden_width), f32),
            jax.ShapeDtypeStruct((1, rows_second, width), f32),
        ]
        * 3,
        compiler_params=pltpu.CompilerParams(vmem_limit_bytes=UPDATE_LIMIT),
    )(info, mine, theirs, *firsts, *seconds, w1, w2, m1, m2, v1, v2)


def after(value, *others):
    return lax.optimization_barrier((value, *others))[0]


def body(
    tokens,
    assigned,
    gate_prob,
    cotangent,
    weight_in,
    weight_out,
    moment_in,
    moment_out,
    second_in,
    second_out,
):
    experts = lax.axis_size("expert")
    replicas = lax.axis_size("dp")
    top = replicas // 2
    self_index = lax.axis_index("dp")
    expert = lax.axis_index("expert")
    half = self_index // top
    member = self_index % top
    tok_rows, width = tokens.shape
    hidden_width = weight_in.shape[2]
    capacity = 2 * tok_rows // experts
    rows_first = width // replicas
    rows_second = hidden_width // replicas
    w_first = weight_in[0]
    w_second = weight_out[0]
    info = jnp.stack([member, self_index, half]).astype(jnp.int32)

    ids = assigned.reshape(-1, 128)
    far_ids = swap(ids, "dp", top)
    scaled = (after(gate_prob, ids) * cotangent.astype(f32)).astype(bf16)
    far_scaled = swap(scaled, "dp", top)
    table = slot_table(assigned, expert, experts, capacity)
    upstream, own_sent = dispatch(table, scaled, experts)
    inputs = dispatch(table, after(tokens, *own_sent), experts)[0]
    far_tokens = swap(after(tokens, upstream), "dp", top)

    far_table = slot_table(far_ids.reshape(-1, 1), expert, experts, capacity)
    own_in, own_out, partial_out = expert_call(
        "first", info, after(inputs, upstream), upstream, w_first, w_second
    )
    far_scaled = after(far_scaled, partial_out)
    far_upstream, far_sent = dispatch(far_table, far_scaled, experts)
    own_in, own_out, partial_out = expert_call(
        "middle",
        info,
        inputs,
        upstream,
        w_first,
        w_second,
        after(partial_out, *far_sent),
        own_in,
        own_out,
    )
    far_tokens = after(far_tokens, partial_out)
    far_inputs, far_sent = dispatch(far_table, far_tokens, experts)
    own_in, expert_out = expert_call(
        "last",
        info,
        inputs,
        upstream,
        w_first,
        w_second,
        after(partial_out, *far_sent),
        own_in,
    )

    expert_out = after(expert_out, far_upstream, far_inputs)
    returned = exchange_blocks(
        [expert_out[j * capacity : (j + 1) * capacity] for j in range(experts)]
    )
    far_in, far_out, mine = expert_call(
        "far", info, far_inputs, far_upstream, w_first, w_second, own_in, own_out
    )
    mine = after(mine, returned)

    theirs = swap(mine, "dp", top)
    cross = mine[0] + theirs[0]
    norm_own = mine[1] + theirs[2]
    norm_far = mine[2] + theirs[1]
    coef_own = 1.0 - cross / (2.0 * (norm_own + eps_adasum))
    coef_far = 1.0 - cross / (2.0 * (norm_far + eps_adasum))
    weighted = coef_own * coef_own * norm_own + coef_far * coef_far * norm_far
    norm = jnp.maximum(weighted + 2.0 * coef_own * coef_far * cross, 1e-5 * weighted)
    scale = 16384.0 * lax.rsqrt(jnp.maximum(norm, 1e-12))
    weight_own, weight_far = coef_own * scale, coef_far * scale

    def quarter(own, far, other, axis, left, right):
        size = own.shape[axis] // top
        own, far = (
            lax.dynamic_slice_in_dim(x, (member ^ other) * size, size, axis) for x in (own, far)
        )
        return left * own + right * far

    def exchange(own, far, axis):
        pair = (weight_own[0], weight_far[0])
        others = range(1, top)
        outgoing = [quarter(own, far, other, axis, *pair).astype(f16) for other in others]
        if axis == 0:
            pair = [after(weight, *outgoing) for weight in pair]
        received = [swap(x, "dp", other).astype(f32) for x, other in zip(outgoing, others)]
        return [quarter(own, far, 0, axis, *pair)] + received

    firsts = exchange(own_in, far_in, 0)
    seconds = exchange(own_out, far_out, 1)

    products = gram_call(info, scale.reshape(1, 128), firsts, True)
    products = gram_call(info, products, seconds, False)
    bit = 1
    while bit < top:
        products = products + swap(products, "dp", bit)
        bit *= 2
    new = update_call(
        info,
        products,
        swap(products, "dp", top),
        firsts,
        seconds,
        weight_in,
        weight_out,
        moment_in,
        moment_out,
        second_in,
        second_out,
    )

    picked = contract_rows(table, jnp.concatenate(returned, axis=0))
    combined = (gate_prob * picked).astype(bf16)
    return (combined, *new)


def solution(mesh):
    row_spec = P(("dp", "expert"), None)
    owner_spec = P("expert", "dp", None)
    return jax.shard_map(
        body,
        mesh=mesh,
        in_specs=(row_spec,) * 4 + (P("expert", None, None),) * 2 + (owner_spec,) * 4,
        out_specs=(row_spec,) + (owner_spec,) * 6,
        check_vma=False,
    )
```
